256 devices in a mesh: arc: 16 (over y, x_lo, core), coef: 16 (over x_hi, z).
Axes of the slice: x: 4 (x_hi: 2, x_lo: 2; x = x_hi * 2 + x_lo), y: 4, z: 8, core: 2. Of those that a mesh axis runs over, the one named last changes fastest.
Arguments:
- design: float32 [8192, 16384], P('arc', 'coef'), may hold values from -0.046875 to 0.046875
- observations: float32 [256, 8192], P('coef', 'arc'), may hold values from -30 to 30, as said below
- start_coefs: float32 [256, 16384], P('arc', 'coef'), may hold values from -3 to 3
- precond: float32 [16384], P('coef'), may hold values from 0.3 to 1.5
- taps: float32 [128], replicated, may hold values from -0.4 to 0.4
Outputs:
- coefs: float32 [256, 16384], P('arc', 'coef')
- misfit: float32 [256, 8192], P('coef', 'arc')
The draws below stay inside these ranges and needn't reach their ends.
Inputs may be any that keep to these rules, and one draw needn't show every extreme that they name: `observations`: observations of a satellite mission with a noise level that varies along time and occasional outliers.
All inputs are finite; a program needn't handle non-finite values.
Results may differ from the reference program's by a relative error of at most 0.00026.
Values sent between devices are 32-bit elements; how exact they have to be, the bound alone decides.
A program may use at most 64 MiB of HBM per device.

```python
import math
import jax
import jax.numpy as jnp
from jax import lax

NCOEF = 16384
NRHS = 256
TAPS = 128
ITERS = 2
NOBS = 8192


def draw_observations(key, part):
    keys = jax.random.split(jax.random.fold_in(key, 11), 4)
    moment = jnp.arange(NOBS, dtype=jnp.float32) / NOBS
    trend = jnp.exp(moment * jnp.log(3.0))
    rough = jnp.exp(jax.random.uniform(keys[1], (NOBS,), minval=-0.7, maxval=0.7))
    base = jax.random.normal(keys[0], (NRHS, NOBS))
    spikes = (jax.random.uniform(keys[2], (NRHS, NOBS)) < 0.02).astype(jnp.float32)
    outliers = spikes * 6.0 * jax.random.normal(keys[3], (NRHS, NOBS))
    values = 0.6 * base * trend[None, :] * rough[None, :] + outliers
    return jnp.clip(values, -30.0, 30.0).astype(jnp.float32)


def block_levels(own_key, extent, cuts, smallest, largest):
    def one(dim, shards_of):
        steps = jax.random.uniform(jax.random.fold_in(jax.random.fold_in(own_key, 6), dim), (shards_of,), jnp.float32, smallest / len(cuts), largest / len(cuts))
        return jnp.repeat(jnp.exp(steps), extent[dim] // shards_of).reshape((-1,) + (1,) * (len(extent) - dim - 1))

    gain = one(*cuts[0])
    for cut in cuts[1:]:
        gain = gain * one(*cut)
    return gain


def centred(key, dims, deviation, bound, pieces=(), kind=jnp.bfloat16):
    values = deviation * jax.random.normal(key, dims, jnp.float32)
    if pieces:
        values = values * block_levels(key, dims, pieces, -0.22, 0.18)
    return jnp.clip(values, -bound, bound).astype(kind)


def setup_inputs(seed: int = 0) -> dict:
    streams_of = jax.random.split(jax.random.key(seed), 6)
    return {
        "design": centred(streams_of[0], (NOBS, NCOEF), NCOEF ** -0.5, 0.046875, ((0, 16), (1, 16)), jnp.float32),
        "observations": draw_observations(jax.random.fold_in(streams_of[5], 71), 0),
        "start_coefs": centred(streams_of[2], (NRHS, NCOEF), 0.5, 3.0, ((0, 16), (1, 16)), jnp.float32),
        "precond": jnp.clip(jnp.exp(math.log(1.5) - 1.60943787 * jax.random.uniform(streams_of[3], (NCOEF,), jnp.float32) ** block_levels(streams_of[3], (NCOEF,), ((0, 16),), -0.2, 0.2)), 0.3, 1.5),
        "taps": centred(streams_of[4], (TAPS,), 0.08, 0.4, (), jnp.float32),
    }


huber_square = 2.25
epsilon = 1e-06

def make_filters(taps):
    filt = taps.at[0].add(1.0)
    source = jnp.arange(TAPS)[:, None]
    target = jnp.arange(TAPS)[None, :]
    offset = target - source
    first = jnp.where(offset >= 0, filt[jnp.clip(offset, 0, TAPS - 1)], 0.0)
    second = jnp.where(offset < 0, filt[jnp.clip(offset + TAPS, 0, TAPS - 1)], 0.0)
    return (first, second)

def whiten(values, edge, first, second):
    blocks = values.reshape(values.shape[0], -1, TAPS)
    before = jnp.concatenate([edge[:, None, :], blocks[:, :-1]], axis=1)
    result = jnp.einsum('kjs,st->kjt', blocks, first, precision=lax.Precision.HIGHEST)
    result = result + jnp.einsum('kjs,st->kjt', before, second, precision=lax.Precision.HIGHEST)
    return result.reshape(values.shape)

def whiten_back(values, edge, first, second):
    blocks = values.reshape(values.shape[0], -1, TAPS)
    after = jnp.concatenate([blocks[:, 1:], edge[:, None, :]], axis=1)
    result = jnp.einsum('kjt,st->kjs', blocks, first, precision=lax.Precision.HIGHEST)
    result = result + jnp.einsum('kjt,st->kjs', after, second, precision=lax.Precision.HIGHEST)
    return result.reshape(values.shape)

def reference(design, observations, start_coefs, precond, taps):
    first, second = make_filters(taps)
    zero_edge = jnp.zeros((NRHS, TAPS), jnp.float32)
    coefs = start_coefs
    predicted = jnp.dot(coefs, design.T, precision=lax.Precision.HIGHEST, preferred_element_type=jnp.float32)
    direction = jnp.zeros_like(coefs)
    previous_gp = jnp.ones((NRHS,), jnp.float32)
    for iteration in range(ITERS):
        residual = observations - predicted
        whitened = whiten(residual, zero_edge, first, second)
        scale = lax.optimization_barrier(jnp.sum(whitened * whitened, axis=1)) / NOBS
        weights = 1.0 / jnp.sqrt(1.0 + whitened * whitened / (huber_square * scale[:, None] + epsilon))
        back = whiten_back(weights * whitened, zero_edge, first, second)
        gradient = jnp.dot(back, design, precision=lax.Precision.HIGHEST, preferred_element_type=jnp.float32)
        conditioned = precond[None, :] * gradient
        grad_prod = lax.optimization_barrier(jnp.sum(gradient * conditioned, axis=1))
        grad_old = lax.optimization_barrier(jnp.sum(gradient * direction, axis=1))
        if iteration == 0:
            direction = conditioned
            grad_dir = grad_prod
        else:
            beta = grad_prod / previous_gp
            direction = conditioned + beta[:, None] * direction
            grad_dir = grad_prod + beta * grad_old
        image = jnp.dot(direction, design.T, precision=lax.Precision.HIGHEST, preferred_element_type=jnp.float32)
        imaged = whiten(image, zero_edge, first, second)
        curvature = lax.optimization_barrier(jnp.sum(weights * imaged * imaged, axis=1))
        alpha = grad_dir / curvature
        coefs = coefs + alpha[:, None] * direction
        predicted = predicted + alpha[:, None] * image
        previous_gp = grad_prod
    return (coefs, observations - predicted)
```

```python
import functools
import jax
import jax.numpy as jnp
from jax import lax
from jax.experimental import pallas as pl
from jax.experimental.pallas import tpu as pltpu
from jax.sharding import PartitionSpec as P

ITERS = 2
TOTAL_OBS = 8192
HUBER_SQUARE = 2.25
EPSILON = 1e-06

F32 = jnp.float32
BF16 = jnp.bfloat16
MESH = pl.DeviceIdType.MESH


def split(value):
    high = value.astype(BF16)
    low = (value - high.astype(F32)).astype(BF16)
    return high, low


def dot3(value, weight_high, weight_low):
    rows = value.shape[0]
    high, low = split(value)
    both = jnp.dot(jnp.concatenate([high, low], axis=0), weight_high, preferred_element_type=F32)
    rest = jnp.dot(high, weight_low, preferred_element_type=F32)
    return both[:rows] + both[rows:] + rest


def lanes(value):
    total = value[:, 0:128]
    for start in range(128, value.shape[1], 128):
        total = total + value[:, start:start + 128]
    return total


def fold(value):
    value = value + pltpu.roll(value, 64, 1)
    lane = lax.broadcasted_iota(jnp.int32, (8, 128), 1)
    return jnp.where(lane < 64, value[0:8], value[8:16])


def unfold(value):
    lane = lax.broadcasted_iota(jnp.int32, (8, 128), 1)
    upper = jnp.sum(jnp.where(lane < 64, value, 0.0), axis=1, keepdims=True)
    lower = jnp.sum(jnp.where(lane < 64, 0.0, value), axis=1, keepdims=True)
    return jnp.concatenate([upper, lower], axis=0)


def filter_blocks(extended):
    return jnp.concatenate([extended[:, j * 128:(j + 2) * 128] for j in range(4)], axis=0)


def unblock(value):
    return jnp.concatenate([value[j * 16:(j + 1) * 16] for j in range(4)], axis=1)


def kernel(design_hbm, obs_ref, start_ref, precond_ref, taps_ref, coefs_ref, misfit_ref,
           design_f, d_high, d_low, t_high, t_low, w_high, w_low, b_high, b_low,
           gather, partial, landed, back_rows, grad_part, pair_land, grad_land,
           edge_src, edge_dst, sum_src, sum_dst, gp_src, gp_dst, diag_gp, diag_alpha,
           load_sem, ag_send, ag_recv, fwd_send, fwd_recv, rs_send, rs_recv,
           bg_send, bg_recv, pair_send, pair_recv, ra_send, ra_recv,
           edge_send, edge_recv, sum_send, sum_recv, gp_send, gp_recv, diag_send, diag_recv):
    a = lax.axis_index("arc")
    c = lax.axis_index("coef")
    y, ma = a // 4, a % 4
    xlo, core = ma // 2, ma % 2
    yc, mc = c // 4, c % 4
    sibling = a + 1 - 2 * core

    load = pltpu.make_async_copy(design_hbm, design_f, load_sem)
    load.start()

    barrier = pltpu.get_barrier_semaphore()

    def greet(k, carry):
        pl.semaphore_signal(barrier, inc=1, device_id=((a + k) % 16, c), device_id_type=MESH)
        pl.semaphore_signal(barrier, inc=1, device_id=(a, (c + k) % 16), device_id_type=MESH)
        return carry

    lax.fori_loop(1, 16, greet, 0)

    def remote(src, dst, send, recv, device):
        return pltpu.make_async_remote_copy(src_ref=src, dst_ref=dst, send_sem=send, recv_sem=recv,
                                            device_id=device, device_id_type=MESH)

    def wait_bytes(ref, sem):
        pltpu.make_async_copy(ref, ref, sem).wait()

    row = lax.broadcasted_iota(jnp.int32, (128, 128), 0)
    col = lax.broadcasted_iota(jnp.int32, (128, 128), 1)
    lead = lax.broadcasted_iota(jnp.int32, (1, 128), 1)
    filt = taps_ref[...] + jnp.where(lead == 0, 1.0, 0.0)
    rolled = jnp.broadcast_to(filt, (128, 128))
    for bit in range(7):
        rolled = jnp.where((row // (1 << bit)) % 2 == 1, pltpu.roll(rolled, 1 << bit, 1), rolled)
    first = jnp.where(col >= row, rolled, 0.0)
    second = jnp.where(col < row, rolled, 0.0)
    high, low = split(jnp.concatenate([second, first], axis=0))
    w_high[...] = high
    w_low[...] = low
    high, low = split(jnp.concatenate([first.T, second.T], axis=0))
    b_high[...] = high
    b_low[...] = low

    gather[0, ma, y] = start_ref[...]

    pl.semaphore_wait(barrier, 30)

    def gather_arc(p):
        def step(k, carry):
            i, ky = k // 4, k % 4
            target = ((y + ky) % 4) * 4 + ((xlo + i) % 2) * 2 + core

            @pl.when(k > 0)
            def _():
                remote(gather.at[p, ma, y], gather.at[p, ma, y], ag_send.at[p], ag_recv.at[p, k], (target, c)).start()
            return carry

        lax.fori_loop(0, 8, step, 0)

    def forward(p):
        def step(s, carry):
            i, j = s // 2, s % 2
            m = ((xlo + i) % 2) * 2 + (core + j) % 2

            @pl.when(j == 0)
            def _():
                for ky in range(4):
                    source_y = (y + 4 - ky) % 4
                    if ky == 0:
                        @pl.when(i > 0)
                        def _():
                            wait_bytes(gather.at[p, m, source_y], ag_recv.at[p, i * 4])
                    else:
                        wait_bytes(gather.at[p, m, source_y], ag_recv.at[p, i * 4 + ky])
                    remote(gather.at[p, m, source_y], gather.at[p, m, source_y], fwd_send.at[p], fwd_recv.at[p, i], (sibling, c)).start()

            @pl.when(j == 1)
            def _():
                wait_bytes(gather.at[p, m], fwd_recv.at[p, i])

            block = gather[p, m].reshape(64, 1024)
            product = dot3(block, t_high[...], t_low[...])
            partial[p, m] = product.reshape(4, 16, 512)
            for k in range(4):
                yk = (yc + k) % 4
                owner = yk * 4 + m

                @pl.when(owner != c)
                def _():
                    remote(partial.at[p, m, yk], landed.at[p, (owner + 16 - c) % 16], rs_send.at[p], rs_recv.at[p], (a, owner)).start()
            return carry

        lax.fori_loop(0, 4, step, 0)

    def forward_sum(p):
        wait_bytes(landed.at[p, 1:16], rs_recv.at[p])
        total = partial[p, mc, yc]
        for k in range(1, 16):
            total = total + landed[p, k]
        return total

    def gather_coef(it):
        def step(k, carry):
            dz, flip = k // 2, k % 2
            dz = (dz // 2) + (dz % 2) * 4
            z, xh = c % 8, c // 8
            target = ((xh + flip) % 2) * 8 + (z + dz) % 8

            @pl.when(k > 0)
            def _():
                remote(back_rows.at[it, mc, yc], back_rows.at[it, mc, yc], bg_send.at[it], bg_recv.at[it, dz % 4], (a, target)).start()
            return carry

        lax.fori_loop(0, 16, step, 0)

    def backward(it):
        def finish(k):
            m = (mc + 4 - k) % 4
            xl, co = m // 2, m % 2

            @pl.when(co == core)
            def _():
                wait_bytes(pair_land.at[it, xl], pair_recv.at[it, xl])
                grad_part[it, m] = grad_part[it, m] + pair_land[it, xl]
                i = (xl + 2 - xlo) % 2
                for ky in range(4):
                    ty = (y + ky) % 4
                    target = ty * 4 + m

                    @pl.when(target != a)
                    def _():
                        remote(grad_part.at[it, m, ty], grad_land.at[it, i * 4 + ky], ra_send.at[it], ra_recv.at[it], (target, c)).start()

        def step(k, carry):
            m = (mc + 4 - k) % 4
            xl, co = m // 2, m % 2

            @pl.when(k == 0)
            def _():
                wait_bytes(back_rows.at[it, m, 0:3], bg_recv.at[it, 0])

            @pl.when(k > 0)
            def _():
                wait_bytes(back_rows.at[it, m], bg_recv.at[it, k])

            block = back_rows[it, m].reshape(64, 512)
            product = dot3(block, d_high[...], d_low[...])
            grad_part[it, m] = product.reshape(4, 16, 1024)

            @pl.when(co != core)
            def _():
                remote(grad_part.at[it, m], pair_land.at[it, xl], pair_send.at[it, xl], pair_recv.at[it, xl], (sibling, c)).start()

            @pl.when(k > 0)
            def _():
                finish(k - 1)
            return carry

        lax.fori_loop(0, 4, step, 0)
        finish(3)

    def backward_sum(it):
        wait_bytes(grad_land.at[it, 1:8], ra_recv.at[it])
        total = grad_part[it, ma, y]
        for k in range(1, 8):
            total = total + grad_land[it, k]
        return total

    def edge_next(n, value):
        edge_src[n] = value

        @pl.when(a < 15)
        def _():
            remote(edge_src.at[n], edge_dst.at[n], edge_send.at[n], edge_recv.at[n], (a + 1, c)).start()

        @pl.when(a == 0)
        def _():
            edge_dst[n] = jnp.zeros((16, 128), F32)

    def edge_next_wait(n):
        @pl.when(a > 0)
        def _():
            wait_bytes(edge_dst.at[n], edge_recv.at[n])
        return edge_dst[n]

    def edge_previous(n, value):
        edge_src[n] = value

        @pl.when(a > 0)
        def _():
            remote(edge_src.at[n], edge_dst.at[n], edge_send.at[n], edge_recv.at[n], (a - 1, c)).start()

        @pl.when(a == 15)
        def _():
            edge_dst[n] = jnp.zeros((16, 128), F32)

    def edge_previous_wait(n):
        @pl.when(a < 15)
        def _():
            wait_bytes(edge_dst.at[n], edge_recv.at[n])
        return edge_dst[n]

    def whiten(n, value):
        edge_next(n, value[:, 384:512])
        edge = edge_next_wait(n)
        blocks = filter_blocks(jnp.concatenate([edge, value], axis=1))
        return unblock(dot3(blocks, w_high[...], w_low[...]))

    def whiten_back(n, value):
        edge_previous(n, value[:, 0:128])
        edge = edge_previous_wait(n)
        blocks = filter_blocks(jnp.concatenate([value, edge], axis=1))
        return unblock(dot3(blocks, b_high[...], b_low[...]))

    def time_sum(n, value):
        sum_src[n] = fold(lanes(value))

        def step(k, carry):
            remote(sum_src.at[n], sum_dst.at[n, k], sum_send.at[n], sum_recv.at[n], ((a + k) % 16, c)).start()
            return carry

        lax.fori_loop(1, 16, step, 0)

    def time_sum_wait(n):
        wait_bytes(sum_dst.at[n, 1:16], sum_recv.at[n])
        total = sum_src[n]
        for k in range(1, 16):
            total = total + sum_dst[n, k]
        return unfold(total)

    def coef_sum(it, product, old):
        gp_src[it, 0:8] = fold(lanes(product))
        gp_src[it, 8:16] = fold(lanes(old))

        def step(k, carry):
            remote(gp_src.at[it], gp_dst.at[it, k], gp_send.at[it], gp_recv.at[it], (a, (c + k) % 16)).start()
            return carry

        lax.fori_loop(1, 16, step, 0)

    def coef_sum_wait(it):
        wait_bytes(gp_dst.at[it, 1:16], gp_recv.at[it])
        total = gp_src[it]
        for k in range(1, 16):
            total = total + gp_dst[it, k]

        @pl.when(a == c)
        def _():
            diag_gp[it] = total

            def step(k, carry):
                remote(diag_gp.at[it], diag_gp.at[it], diag_send.at[it, 0], diag_recv.at[it, 0], ((a + k) % 16, c)).start()
                return carry

            lax.fori_loop(1, 16, step, 0)
        return unfold(total[0:8]), unfold(total[8:16])

    def diag_gp_wait(it):
        @pl.when(a != c)
        def _():
            wait_bytes(diag_gp.at[it], diag_recv.at[it, 0])
        total = diag_gp[it]
        return unfold(total[0:8]), unfold(total[8:16])

    def alpha_spread(it, alpha):
        @pl.when(a == c)
        def _():
            diag_alpha[it] = jnp.broadcast_to(alpha, (16, 128))

            def step(k, carry):
                remote(diag_alpha.at[it], diag_alpha.at[it], diag_send.at[it, 1], diag_recv.at[it, 1], (a, (c + k) % 16)).start()
                return carry

            lax.fori_loop(1, 16, step, 0)

    def alpha_wait(it):
        @pl.when(a != c)
        def _():
            wait_bytes(diag_alpha.at[it], diag_recv.at[it, 1])
        return diag_alpha[it][:, 0:1]

    gather_arc(0)

    load.wait()

    def prepare(r, carry):
        at = pl.ds(pl.multiple_of(r * 128, 128), 128)
        piece = design_f[at, :]
        high, low = split(piece)
        d_high[at, :] = high
        d_low[at, :] = low
        high, low = split(piece.T)
        t_high[:, at] = high
        t_low[:, at] = low
        return carry

    lax.fori_loop(0, 4, prepare, 0)

    forward(0)
    observations = obs_ref[...]
    residual = observations - forward_sum(0)
    whitened = whiten(0, residual)
    time_sum(0, whitened * whitened)

    image_old = imaged_old = gp_a_old = gp_c_old = None
    betas, alphas = [], []
    for it in range(ITERS):
        scale = time_sum_wait(2 * it) * (1.0 / TOTAL_OBS)
        weights = lax.rsqrt(1.0 + whitened * whitened / (HUBER_SQUARE * scale + EPSILON))
        back = whiten_back(1 + 2 * it, weights * whitened)
        back_rows[it, mc, yc] = back
        gather_coef(it)
        backward(it)
        gradient = backward_sum(it)
        conditioned = precond_ref[...] * gradient
        gather[it + 1, ma, y] = conditioned
        gather_arc(it + 1)
        if it == 0:
            old = jnp.zeros_like(gradient)
        else:
            old = gradient * direction
        coef_sum(it, gradient * conditioned, old)
        forward(it + 1)
        gp_a, go_a = coef_sum_wait(it)
        if it == 0:
            direction = conditioned
        else:
            direction = conditioned + (gp_a / gp_a_old) * direction
        image = forward_sum(it + 1)
        imaged = whiten(2 + 2 * it, image)
        gp_c, go_c = diag_gp_wait(it)
        if it == 0:
            gd_c = gp_c
        else:
            beta_c = gp_c / gp_c_old
            gd_c = gp_c + beta_c * go_c
            image = image + beta_c * image_old
            imaged = imaged + beta_c * imaged_old
        time_sum(2 * it + 1, weights * imaged * imaged)
        alpha = gd_c / time_sum_wait(2 * it + 1)
        alpha_spread(it, alpha)
        residual = residual - alpha * image
        if it + 1 < ITERS:
            whitened = whitened - alpha * imaged
            time_sum(2 * it + 2, whitened * whitened)
        image_old, imaged_old, gp_a_old, gp_c_old = image, imaged, gp_a, gp_c
        if it == 0:
            first_direction = direction
    misfit_ref[...] = residual
    coefs = start_ref[...]
    coefs = coefs + alpha_wait(0) * first_direction
    coefs = coefs + alpha_wait(1) * direction
    coefs_ref[...] = coefs

    for p in range(ITERS + 1):
        wait_bytes(landed.at[p, 0:14], ag_send.at[p])
        wait_bytes(gather.at[p, 0:2], fwd_send.at[p])
        wait_bytes(landed.at[p, 1:16], rs_send.at[p])
    for it in range(ITERS):
        wait_bytes(landed.at[it, 1:16], bg_send.at[it])
        for xl in range(2):
            wait_bytes(pair_land.at[it, xl], pair_send.at[it, xl])
        wait_bytes(grad_land.at[it, 1:8], ra_send.at[it])
        wait_bytes(gp_dst.at[it, 1:16], gp_send.at[it])

        @pl.when(a == c)
        def _():
            wait_bytes(gp_dst.at[it, 1:16], diag_send.at[it, 0])
            wait_bytes(gp_dst.at[it, 1:16], diag_send.at[it, 1])
    for n in range(2 * ITERS):
        wait_bytes(sum_dst.at[n, 1:16], sum_send.at[n])
    for n in range(2 * ITERS + 1):
        @pl.when((a < 15) if n % 2 == 0 else (a > 0))
        def _():
            wait_bytes(edge_src.at[n], edge_send.at[n])


def body(design, observations, start_coefs, precond, taps):
    vmem = pl.BlockSpec(memory_space=pltpu.VMEM)
    dma = pltpu.SemaphoreType.DMA
    scratch = [
        pltpu.VMEM((512, 1024), F32),
        pltpu.VMEM((512, 1024), BF16), pltpu.VMEM((512, 1024), BF16),
        pltpu.VMEM((1024, 512), BF16), pltpu.VMEM((1024, 512), BF16),
        pltpu.VMEM((256, 128), BF16), pltpu.VMEM((256, 128), BF16),
        pltpu.VMEM((256, 128), BF16), pltpu.VMEM((256, 128), BF16),
        pltpu.VMEM((3, 4, 4, 16, 1024), F32),
        pltpu.VMEM((3, 4, 4, 16, 512), F32),
        pltpu.VMEM((3, 16, 16, 512), F32),
        pltpu.VMEM((2, 4, 4, 16, 512), F32),
        pltpu.VMEM((2, 4, 4, 16, 1024), F32),
        pltpu.VMEM((2, 2, 4, 16, 1024), F32),
        pltpu.VMEM((2, 8, 16, 1024), F32),
        pltpu.VMEM((5, 16, 128), F32), pltpu.VMEM((5, 16, 128), F32),
        pltpu.VMEM((4, 8, 128), F32), pltpu.VMEM((4, 16, 8, 128), F32),
        pltpu.VMEM((2, 16, 128), F32), pltpu.VMEM((2, 16, 16, 128), F32),
        pltpu.VMEM((2, 16, 128), F32), pltpu.VMEM((2, 16, 128), F32),
        dma,
        dma((3,)), dma((3, 8)), dma((3,)), dma((3, 2)), dma((3,)), dma((3,)),
        dma((2,)), dma((2, 4)), dma((2, 2)), dma((2, 2)), dma((2,)), dma((2,)),
        dma((5,)), dma((5,)), dma((4,)), dma((4,)), dma((2,)), dma((2,)), dma((2, 2)), dma((2, 2)),
    ]
    return pl.pallas_call(
        kernel,
        out_shape=(jax.ShapeDtypeStruct(start_coefs.shape, F32), jax.ShapeDtypeStruct(observations.shape, F32)),
        in_specs=[pl.BlockSpec(memory_space=pl.ANY), vmem, vmem, vmem, vmem],
        out_specs=(vmem, vmem),
        scratch_shapes=scratch,
        compiler_params=pltpu.CompilerParams(collective_id=0, has_side_effects=True, vmem_limit_bytes=48 << 20),
    )(design, observations, start_coefs, precond.reshape(1, -1), taps.reshape(1, -1))


def solution(mesh):
    placed = (P("arc", "coef"), P("coef", "arc"), P("arc", "coef"), P("coef"), P())
    return jax.shard_map(
        body,
        mesh=mesh,
        in_specs=placed,
        out_specs=(P("arc", "coef"), P("coef", "arc")),
        check_vma=False,
    )
```

```python
import functools
import jax
import jax.numpy as jnp
from jax import lax
from jax.experimental import pallas as pl
from jax.experimental.pallas import tpu as pltpu
from jax.sharding import PartitionSpec as P

ITERS = 2
TOTAL_OBS = 8192
HUBER_SQUARE = 2.25
EPSILON = 1e-06

F32 = jnp.float32
BF16 = jnp.bfloat16
MESH = pl.DeviceIdType.MESH


def split(value):
    high = value.astype(BF16)
    low = (value - high.astype(F32)).astype(BF16)
    return high, low


def dot3(value, weight_high, weight_low):
    rows = value.shape[0]
    high, low = split(value)
    both = jnp.dot(jnp.concatenate([high, low], axis=0), weight_high, preferred_element_type=F32)
    rest = jnp.dot(high, weight_low, preferred_element_type=F32)
    return both[:rows] + both[rows:] + rest


def lanes(value):
    total = value[:, 0:128]
    for start in range(128, value.shape[1], 128):
        total = total + value[:, start:start + 128]
    return total


def fold(values):
    group = lax.broadcasted_iota(jnp.int32, (8, 128), 1) // 16
    tile = jnp.zeros((8, 128), F32)
    for n, value in enumerate(values):
        for shift in (64, 32, 16):
            value = value + pltpu.roll(value, shift, 1)
        tile = jnp.where(group == 2 * n, value[0:8], tile)
        tile = jnp.where(group == 2 * n + 1, value[8:16], tile)
    return tile


def unfold(tile, count):
    for shift in (8, 4, 2, 1):
        tile = tile + pltpu.roll(tile, shift, 1)
    return [jnp.concatenate([tile[:, 32 * n + 15:32 * n + 16], tile[:, 32 * n + 31:32 * n + 32]], axis=0) for n in range(count)]


def pack(one, two):
    lane = lax.broadcasted_iota(jnp.int32, (8, 128), 1)
    return jnp.where(lane < 64, jnp.where(lane < 32, one[0:8], one[8:16]), jnp.where(lane < 96, two[0:8], two[8:16]))


def unpack(tile, which):
    start = 64 * which
    return jnp.concatenate([tile[:, start:start + 1], tile[:, start + 32:start + 33]], axis=0)


def filter_blocks(extended):
    return jnp.concatenate([extended[:, j * 128:(j + 2) * 128] for j in range(4)], axis=0)


def unblock(value):
    return jnp.concatenate([value[j * 16:(j + 1) * 16] for j in range(4)], axis=1)


def kernel(design_hbm, obs_hbm, start_hbm, precond_hbm, taps_hbm, coefs_ref, misfit_ref,
           design_f, obs_v, precond_v, taps_v, halo, d_high, d_low, g_high, g_low, t_high, t_low, w_high, w_low, filter_t,
           gather, partial, pair_part, landed, back_rows, grad_part, pair_land, grad_land,
           edge_src, edge_dst, sum_src, sum_dst, gp_src, gp_dst, diag_gp, diag_alpha, vector,
           load_sem, halo_sem, ag_send, ag_recv, fwd_send, fwd_recv, part_send, part_recv, rs_send, rs_recv,
           bg_send, bg_recv, bf_send, bf_recv, pair_send, pair_recv, ra_send, ra_recv,
           edge_send, edge_recv, sum_send, sum_recv, gp_send, gp_recv, diag_send, diag_recv, vec_send, vec_recv):
    a = lax.axis_index("arc")
    c = lax.axis_index("coef")
    y, ma = a // 4, a % 4
    xlo, core = ma // 2, ma % 2
    yc, mc = c // 4, c % 4
    xh, z = c // 8, c % 8
    sibling = a + 1 - 2 * core
    across = (xh * 8 + 8) % 16 + z

    loads = []
    for n, (source, target) in enumerate([(start_hbm, gather.at[0, ma, y]), (taps_hbm, taps_v), (design_hbm, design_f),
                                          (obs_hbm, obs_v), (precond_hbm, precond_v)]):
        loads.append(pltpu.make_async_copy(source, target, load_sem.at[n]))
        loads[-1].start()

    barrier = pltpu.get_barrier_semaphore()

    def greet(k, carry):
        pl.semaphore_signal(barrier, inc=1, device_id=((a + k) % 16, c), device_id_type=MESH)
        pl.semaphore_signal(barrier, inc=1, device_id=(a, (c + k) % 16), device_id_type=MESH)
        return carry

    lax.fori_loop(1, 16, greet, 0)

    def remote(src, dst, send, recv, device):
        return pltpu.make_async_remote_copy(src_ref=src, dst_ref=dst, send_sem=send, recv_sem=recv,
                                            device_id=device, device_id_type=MESH)

    def wait_bytes(ref, sem):
        pltpu.make_async_copy(ref, ref, sem).wait()

    pending = []

    def later(ref, sem, condition=None):
        pending.append((ref, sem, condition))

    def drain():
        for ref, sem, condition in pending:
            if condition is None:
                wait_bytes(ref, sem)
            else:
                pl.when(condition)(functools.partial(wait_bytes, ref, sem))

    loads[1].wait()
    row = lax.broadcasted_iota(jnp.int32, (128, 128), 0)
    col = lax.broadcasted_iota(jnp.int32, (128, 128), 1)
    lead = lax.broadcasted_iota(jnp.int32, (1, 128), 1)
    filt = taps_v[...] + jnp.where(lead == 0, 1.0, 0.0)
    rolled = jnp.broadcast_to(filt, (128, 128))
    for bit in range(7):
        rolled = jnp.where((row // (1 << bit)) % 2 == 1, pltpu.roll(rolled, 1 << bit, 1), rolled)
    first = jnp.where(col >= row, rolled, 0.0)
    second = jnp.where(col < row, rolled, 0.0)
    high, low = split(jnp.concatenate([second, first], axis=0))
    w_high[...] = high
    w_low[...] = low
    high, low = split(jnp.concatenate([second.T, first.T], axis=1))
    filter_t[...] = jnp.concatenate([high, low], axis=0)

    loads[0].wait()
    pl.semaphore_wait(barrier, 30)

    def along_y(p, m, i):
        for ky in (1, 3, 2):
            target = ((y + ky) % 4) * 4 + ma
            remote(gather.at[p, m, y], gather.at[p, m, y], ag_send.at[p], ag_recv.at[p, i * 4 + ky], (target, c)).start()

    def gather_arc(p):
        own = gather.at[p, ma, y]
        remote(own, own, ag_send.at[p], ag_recv.at[p, 4], (y * 4 + (ma + 2) % 4, c)).start()
        along_y(p, ma, 0)
        remote(own, own, fwd_send.at[p], fwd_recv.at[p, 0], (sibling, c)).start()
        later(landed.at[0:2, 0:7], ag_send.at[p])

    def forward(p):
        wait_bytes(gather.at[p, (ma + 2) % 4, y], ag_recv.at[p, 4])
        along_y(p, (ma + 2) % 4, 1)

        def block_of(s):
            return ((xlo + s // 2) % 2) * 2 + (core + s % 2) % 2

        def finish(s):
            m = block_of(s)
            wait_bytes(pair_part.at[p, m], part_recv.at[p, m])
            for h in range(2):
                at = 2 * xh + h
                partial[p, m, at] = partial[p, m, at] + pair_part[p, m, h]

                @pl.when(4 * h + m != z)
                def _():
                    remote(partial.at[p, m, at], landed.at[p, (4 * h + m + 8 - z) % 8], rs_send.at[p], rs_recv.at[p],
                           (a, xh * 8 + 4 * h + m)).start()

        def step(s, carry):
            i, j = s // 2, s % 2
            m = block_of(s)

            @pl.when(j == 0)
            def _():
                for ky in range(4):
                    block = gather.at[p, m, (y + 4 - ky) % 4]
                    if ky == 0:
                        @pl.when(i > 0)
                        def _():
                            remote(block, block, fwd_send.at[p], fwd_recv.at[p, i], (sibling, c)).start()
                    else:
                        wait_bytes(block, ag_recv.at[p, i * 4 + ky])
                        remote(block, block, fwd_send.at[p], fwd_recv.at[p, i], (sibling, c)).start()

            @pl.when(j == 1)
            def _():
                wait_bytes(gather.at[p, m], fwd_recv.at[p, i])

            product = dot3(gather[p, m].reshape(64, 1024), t_high[...], t_low[...])
            partial[p, m] = product.reshape(4, 16, 512)
            remote(partial.at[p, m, pl.ds(2 - 2 * xh, 2)], pair_part.at[p, m], part_send.at[p], part_recv.at[p, m], (a, across)).start()

            @pl.when(s >= 2)
            def _():
                finish(s - 2)
            return carry

        lax.fori_loop(0, 4, step, 0)
        finish(2)
        finish(3)
        later(gather.at[p, 0:2], fwd_send.at[p])
        later(pair_part.at[p], part_send.at[p])
        later(landed.at[p, 1:8], rs_send.at[p])

    def forward_sum(p):
        wait_bytes(landed.at[p, 1:8], rs_recv.at[p])
        total = partial[p, mc, yc]
        for k in range(1, 8):
            total = total + landed[p, k]
        return total

    def gather_coef(it):
        own = back_rows.at[it, mc, yc]
        remote(own, own, bf_send.at[it], bf_recv.at[it], (a, across)).start()
        for dz in (1, 7, 2, 6, 3, 5, 4):
            remote(own, own, bg_send.at[it], bg_recv.at[it, dz], (a, xh * 8 + (z + dz) % 8)).start()

    def gather_coef_on(it):
        for dz in (1, 7, 2, 6, 3, 5, 4):
            source = (z + 8 - dz) % 8
            block = back_rows.at[it, source % 4, 2 * xh + source // 4]
            wait_bytes(block, bg_recv.at[it, dz])
            remote(block, block, bf_send.at[it], bf_recv.at[it], (a, across)).start()
        wait_bytes(back_rows.at[it, 0:2], bf_recv.at[it])
        later(landed.at[it, 1:8], bg_send.at[it])
        later(back_rows.at[it, 0:2], bf_send.at[it])

    def spread(it, one, two):
        own = vector.at[it, mc, yc]
        own[...] = pack(one, two)

        def step(k, carry):
            remote(own, own, vec_send.at[it], vec_recv.at[it], (a, (c + k) % 16)).start()
            return carry

        lax.fori_loop(1, 16, step, 0)
        later(sum_dst.at[it, 1:16], vec_send.at[it])

    def spread_wait(it):
        wait_bytes(sum_dst.at[it, 1:16], vec_recv.at[it])

    def spread_rows(it, m, which):
        return jnp.concatenate([unpack(vector[it, m, k], which) for k in range(4)], axis=0)

    def weighted_rows(it, m):
        rows = back_rows[0, m].reshape(64, 512)
        if it == 0:
            return rows * lax.rsqrt(1.0 + rows * rows * spread_rows(0, m, 0))
        rows = rows - spread_rows(1, m, 0) * back_rows[1, m].reshape(64, 512)
        return rows * lax.rsqrt(1.0 + rows * rows * spread_rows(1, m, 1))

    def backward(it):
        def finish(i):
            xl = (xlo + i) % 2
            m = 2 * xl + core
            wait_bytes(pair_land.at[it, xl], pair_recv.at[it, xl])
            grad_part[it, m] = grad_part[it, m] + pair_land[it, xl]
            for ky in (1, 3, 2, 0):
                ty = (y + ky) % 4
                if ky == 0 and i == 0:
                    continue
                remote(grad_part.at[it, m, ty], grad_land.at[it, i * 4 + ky], ra_send.at[it], ra_recv.at[it], (ty * 4 + m, c)).start()

        def step(s, carry):
            i, j = 1 - s // 2, 1 - s % 2
            xl = (xlo + i) % 2
            m = 2 * xl + (core + j) % 2
            product = dot3(weighted_rows(it, m), g_high[...], g_low[...])
            grad_part[it, m] = product.reshape(4, 16, 1024)

            @pl.when(j == 1)
            def _():
                remote(grad_part.at[it, m], pair_land.at[it, xl], pair_send.at[it, xl], pair_recv.at[it, xl], (sibling, c)).start()

            @pl.when(s == 2)
            def _():
                finish(1)
            return carry

        lax.fori_loop(0, 4, step, 0)
        finish(0)
        for xl in range(2):
            later(pair_land.at[it, xl], pair_send.at[it, xl])
        later(grad_land.at[it, 1:8], ra_send.at[it])

    def backward_sum(it):
        wait_bytes(grad_land.at[it, 1:8], ra_recv.at[it])
        total = grad_part[it, ma, y]
        for k in range(1, 8):
            total = total + grad_land[it, k]
        return total

    def whiten(n, value):
        edge_src[n] = value[:, 384:512]

        @pl.when(a < 15)
        def _():
            remote(edge_src.at[n], edge_dst.at[n], edge_send.at[n], edge_recv.at[n], (a + 1, c)).start()

        later(edge_src.at[n], edge_send.at[n], a < 15)

        @pl.when(a == 0)
        def _():
            edge_dst[n] = jnp.zeros((16, 128), F32)

        inside = filter_blocks(jnp.concatenate([jnp.zeros((16, 128), F32), value], axis=1))
        inside = unblock(dot3(inside, w_high[...], w_low[...]))

        @pl.when(a > 0)
        def _():
            wait_bytes(edge_dst.at[n], edge_recv.at[n])

        outside = dot3(edge_dst[n], w_high[0:128, :], w_low[0:128, :])
        return jnp.concatenate([inside[:, 0:128] + outside, inside[:, 128:512]], axis=1)

    def time_sum(n, values):
        sum_src[n] = fold([lanes(value) for value in values])

        def step(k, carry):
            remote(sum_src.at[n], sum_dst.at[n, k], sum_send.at[n], sum_recv.at[n], ((a + k) % 16, c)).start()
            return carry

        lax.fori_loop(1, 16, step, 0)
        later(sum_dst.at[n, 1:16], sum_send.at[n])

    def time_sum_wait(n, count):
        wait_bytes(sum_dst.at[n, 1:16], sum_recv.at[n])
        total = sum_src[n]
        for k in range(1, 16):
            total = total + sum_dst[n, k]
        return unfold(total, count)

    def coef_sum(it, product, old):
        gp_src[it] = fold([lanes(product), lanes(old)])

        def step(k, carry):
            remote(gp_src.at[it], gp_dst.at[it, k], gp_send.at[it], gp_recv.at[it], (a, (c + k) % 16)).start()
            return carry

        lax.fori_loop(1, 16, step, 0)
        later(gp_dst.at[it, 1:16], gp_send.at[it])

    def coef_sum_wait(it):
        wait_bytes(gp_dst.at[it, 1:16], gp_recv.at[it])
        total = gp_src[it]
        for k in range(1, 16):
            total = total + gp_dst[it, k]

        @pl.when(a == c)
        def _():
            diag_gp[it] = total

            def step(k, carry):
                remote(diag_gp.at[it], diag_gp.at[it], diag_send.at[it], diag_recv.at[it], ((a + k) % 16, c)).start()
                return carry

            lax.fori_loop(1, 16, step, 0)
        later(gp_dst.at[it, 1:16], diag_send.at[it], a == c)
        return unfold(total, 2)

    def diag_gp_wait(it):
        @pl.when(a != c)
        def _():
            wait_bytes(diag_gp.at[it], diag_recv.at[it])
        return unfold(diag_gp[it], 2)

    def alpha_spread(alpha):
        @pl.when(a == c)
        def _():
            diag_alpha[...] = pack(alpha, alpha)

            def step(k, carry):
                remote(diag_alpha, diag_alpha, diag_send.at[ITERS], diag_recv.at[ITERS], (a, (c + k) % 16)).start()
                return carry

            lax.fori_loop(1, 16, step, 0)
        later(gp_dst.at[0, 1:16], diag_send.at[ITERS], a == c)

    def alpha_wait():
        @pl.when(a != c)
        def _():
            wait_bytes(diag_alpha, diag_recv.at[ITERS])
        return unpack(diag_alpha[...], 0)

    gather_arc(0)
    loads[2].wait()

    @pl.when(a < 15)
    def _():
        remote(design_f.at[384:512], halo, halo_sem.at[0], halo_sem.at[1], (a + 1, c)).start()

    later(halo, halo_sem.at[0], a < 15)

    @pl.when(a == 0)
    def _():
        halo[...] = jnp.zeros((128, 1024), F32)

    def prepare(r, carry):
        at = pl.ds(pl.multiple_of(r * 128, 128), 128)
        piece = design_f[at, :]
        high, low = split(piece)
        d_high[pl.ds(pl.multiple_of(r * 128 + 128, 128), 128), :] = high
        d_low[pl.ds(pl.multiple_of(r * 128 + 128, 128), 128), :] = low
        high, low = split(piece.T)
        t_high[:, at] = high
        t_low[:, at] = low
        return carry

    lax.fori_loop(0, 4, prepare, 0)
    forward(0)

    @pl.when(a > 0)
    def _():
        wait_bytes(halo, halo_sem.at[1])

    high, low = split(halo[...])
    d_high[0:128, :] = high
    d_low[0:128, :] = low

    def whiten_design(r, carry):
        at = pl.ds(pl.multiple_of(r * 128, 128), 256)
        both = jnp.dot(filter_t[...], d_high[at, :], preferred_element_type=F32)
        rest = jnp.dot(filter_t[0:128, :], d_low[at, :], preferred_element_type=F32)
        high, low = split(both[0:128] + both[128:256] + rest)
        g_high[pl.ds(pl.multiple_of(r * 128, 128), 128), :] = high
        g_low[pl.ds(pl.multiple_of(r * 128, 128), 128), :] = low
        return carry

    lax.fori_loop(0, 4, whiten_design, 0)
    loads[3].wait()
    loads[4].wait()
    residual = obs_v[...] - forward_sum(0)
    whitened = whiten(0, residual)
    time_sum(0, [whitened * whitened])
    back_rows[0, mc, yc] = whitened
    gather_coef(0)
    square, = time_sum_wait(0, 1)
    factor = 1.0 / (square * (HUBER_SQUARE / TOTAL_OBS) + EPSILON)
    spread(0, factor, factor)

    for it in range(ITERS):
        weights = lax.rsqrt(1.0 + whitened * whitened * factor)
        gather_coef_on(it)
        spread_wait(it)
        backward(it)
        gradient = backward_sum(it)
        conditioned = precond_v[...] * gradient
        gather[it + 1, ma, y] = conditioned
        gather_arc(it + 1)
        if it == 0:
            coef_sum(it, gradient * conditioned, gradient)
        else:
            coef_sum(it, gradient * conditioned, gradient * direction)
        forward(it + 1)
        gp_a, go_a = coef_sum_wait(it)
        if it == 0:
            first_direction = direction = conditioned
        else:
            direction = conditioned + (gp_a / gp_a_old) * direction
        image = forward_sum(it + 1)
        imaged = whiten(it + 1, image)
        gp_c, go_c = diag_gp_wait(it)
        if it == 0:
            time_sum(1, [weights * imaged * imaged, whitened * imaged, imaged * imaged])
            back_rows[1, mc, yc] = imaged
            gather_coef(1)
            curvature, cross, own = time_sum_wait(1, 3)
            alpha = gp_c / curvature
            square = jnp.maximum(square - 2.0 * alpha * cross + alpha * alpha * own, 0.0)
            factor = 1.0 / (square * (HUBER_SQUARE / TOTAL_OBS) + EPSILON)
            spread(1, alpha, factor)
            whitened = whitened - alpha * imaged
            gp_a_old, gp_c_old, image_old, imaged_old = gp_a, gp_c, image, imaged
        else:
            beta = gp_c / gp_c_old
            image = image + beta * image_old
            imaged = imaged + beta * imaged_old
            time_sum(2, [weights * imaged * imaged])
            curvature, = time_sum_wait(2, 1)
            alpha = (gp_c + beta * go_c) / curvature
            alpha_spread(alpha)
        residual = residual - alpha * image
    misfit_ref[...] = residual
    coefs = gather[0, ma, y] + unpack(vector[1, ma, y], 0) * first_direction
    coefs_ref[...] = coefs + alpha_wait() * direction
    drain()


def body(design, observations, start_coefs, precond, taps):
    vmem = pl.BlockSpec(memory_space=pltpu.VMEM)
    dma = pltpu.SemaphoreType.DMA
    scratch = [
        pltpu.VMEM((512, 1024), F32), pltpu.VMEM((16, 512), F32), pltpu.VMEM((1, 1024), F32), pltpu.VMEM((1, 128), F32),
        pltpu.VMEM((128, 1024), F32),
        pltpu.VMEM((640, 1024), BF16), pltpu.VMEM((640, 1024), BF16),
        pltpu.VMEM((512, 1024), BF16), pltpu.VMEM((512, 1024), BF16),
        pltpu.VMEM((1024, 512), BF16), pltpu.VMEM((1024, 512), BF16),
        pltpu.VMEM((256, 128), BF16), pltpu.VMEM((256, 128), BF16), pltpu.VMEM((256, 256), BF16),
        pltpu.VMEM((3, 4, 4, 16, 1024), F32),
        pltpu.VMEM((3, 4, 4, 16, 512), F32),
        pltpu.VMEM((3, 4, 2, 16, 512), F32),
        pltpu.VMEM((3, 8, 16, 512), F32),
        pltpu.VMEM((2, 4, 4, 16, 512), F32),
        pltpu.VMEM((2, 4, 4, 16, 1024), F32),
        pltpu.VMEM((2, 2, 4, 16, 1024), F32),
        pltpu.VMEM((2, 8, 16, 1024), F32),
        pltpu.VMEM((3, 16, 128), F32), pltpu.VMEM((3, 16, 128), F32),
        pltpu.VMEM((3, 8, 128), F32), pltpu.VMEM((3, 16, 8, 128), F32),
        pltpu.VMEM((2, 8, 128), F32), pltpu.VMEM((2, 16, 8, 128), F32),
        pltpu.VMEM((2, 8, 128), F32), pltpu.VMEM((8, 128), F32),
        pltpu.VMEM((2, 4, 4, 8, 128), F32),
        dma((5,)), dma((2,)),
        dma((3,)), dma((3, 8)), dma((3,)), dma((3, 2)), dma((3,)), dma((3, 4)), dma((3,)), dma((3,)),
        dma((2,)), dma((2, 8)), dma((2,)), dma((2,)), dma((2, 2)), dma((2, 2)), dma((2,)), dma((2,)),
        dma((3,)), dma((3,)), dma((3,)), dma((3,)), dma((2,)), dma((2,)), dma((3,)), dma((3,)), dma((2,)), dma((2,)),
    ]
    return pl.pallas_call(
        kernel,
        out_shape=(jax.ShapeDtypeStruct(start_coefs.shape, F32), jax.ShapeDtypeStruct(observations.shape, F32)),
        in_specs=[pl.BlockSpec(memory_space=pl.ANY)] * 5,
        out_specs=(vmem, vmem),
        scratch_shapes=scratch,
        compiler_params=pltpu.CompilerParams(collective_id=0, has_side_effects=True, vmem_limit_bytes=60 << 20),
    )(design, observations, start_coefs, precond.reshape(1, -1), taps.reshape(1, -1))


def solution(mesh):
    placed = (P("arc", "coef"), P("coef", "arc"), P("arc", "coef"), P("coef"), P())
    return jax.shard_map(
        body,
        mesh=mesh,
        in_specs=placed,
        out_specs=(P("arc", "coef"), P("coef", "arc")),
        check_vma=False,
    )
```

```python
import functools
import jax
import jax.numpy as jnp
from jax import lax
from jax.experimental import pallas as pl
from jax.experimental.pallas import tpu as pltpu
from jax.sharding import PartitionSpec as P

ITERS = 2
TOTAL_OBS = 8192
HUBER_SQUARE = 2.25
EPSILON = 1e-06

F32 = jnp.float32
BF16 = jnp.bfloat16
MESH = pl.DeviceIdType.MESH


def split(value):
    high = value.astype(BF16)
    low = (value - high.astype(F32)).astype(BF16)
    return high, low


def dot3(value, weight_high, weight_low):
    rows = value.shape[0]
    high, low = split(value)
    both = jnp.dot(jnp.concatenate([high, low], axis=0), weight_high, preferred_element_type=F32)
    rest = jnp.dot(high, weight_low, preferred_element_type=F32)
    return both[:rows] + both[rows:] + rest


def lanes(value):
    total = value[:, 0:128]
    for start in range(128, value.shape[1], 128):
        total = total + value[:, start:start + 128]
    return total


def fold(values):
    group = lax.broadcasted_iota(jnp.int32, (8, 128), 1) // 16
    tile = jnp.zeros((8, 128), F32)
    for n, value in enumerate(values):
        for shift in (64, 32, 16):
            value = value + pltpu.roll(value, shift, 1)
        tile = jnp.where(group == 2 * n, value[0:8], tile)
        tile = jnp.where(group == 2 * n + 1, value[8:16], tile)
    return tile


def unfold(tile, count):
    for shift in (8, 4, 2, 1):
        tile = tile + pltpu.roll(tile, shift, 1)
    return [jnp.concatenate([tile[:, 32 * n + 15:32 * n + 16], tile[:, 32 * n + 31:32 * n + 32]], axis=0) for n in range(count)]


def pack(one, two):
    lane = lax.broadcasted_iota(jnp.int32, (8, 128), 1)
    return jnp.where(lane < 64, jnp.where(lane < 32, one[0:8], one[8:16]), jnp.where(lane < 96, two[0:8], two[8:16]))


def unpack(tile, which):
    start = 64 * which
    return jnp.concatenate([tile[:, start:start + 1], tile[:, start + 32:start + 33]], axis=0)


def filter_blocks(extended):
    return jnp.concatenate([extended[:, j * 128:(j + 2) * 128] for j in range(4)], axis=0)


def unblock(value):
    return jnp.concatenate([value[j * 16:(j + 1) * 16] for j in range(4)], axis=1)


def kernel(design_hbm, obs_hbm, start_hbm, precond_hbm, taps_hbm, coefs_ref, misfit_ref,
           design_f, obs_v, precond_v, taps_v, halo, d_high, d_low, g_f, g_s, g_high, g_low, t_high, t_low, w_high, w_low, filter_t,
           gather, partial, pair_part, landed, own_rows, back_rows, grad_part, grad_land,
           edge_src, edge_dst, sum_src, sum_dst, gp_src, gp_dst, diag_gp, cur_dst, vector,
           load_sem, halo_sem, design_sem, cur_send, cur_recv, ag_send, ag_recv, fwd_send, fwd_recv, part_send, part_recv, rs_send, rs_recv,
           bg_send, bg_recv, bf_send, bf_recv, ra_send, ra_recv,
           edge_send, edge_recv, sum_send, sum_recv, gp_send, gp_recv, diag_send, diag_recv, vec_send, vec_recv):
    a = lax.axis_index("arc")
    c = lax.axis_index("coef")
    y, ma = a // 4, a % 4
    xlo, core = ma // 2, ma % 2
    xh, z = c // 8, c % 8
    yc, mc = c // 4, c % 4
    xlc, side = mc // 2, mc % 2
    sibling = a + 1 - 2 * core
    home = core == side
    across = (xh * 8 + 8) % 16 + z

    loads = []
    for n, (source, target) in enumerate([(start_hbm, gather.at[0, ma, y]), (taps_hbm, taps_v), (design_hbm, design_f),
                                          (obs_hbm, obs_v), (precond_hbm, precond_v)]):
        loads.append(pltpu.make_async_copy(source, target, load_sem.at[n]))
        loads[-1].start()

    barrier = pltpu.get_barrier_semaphore()

    def greet(k, carry):
        pl.semaphore_signal(barrier, inc=1, device_id=((a + k) % 16, c), device_id_type=MESH)
        pl.semaphore_signal(barrier, inc=1, device_id=(a, (c + k) % 16), device_id_type=MESH)
        return carry

    lax.fori_loop(1, 16, greet, 0)

    def greet_z(k, carry):
        pl.semaphore_signal(barrier, inc=1, device_id=(sibling, xh * 8 + (z + k) % 8), device_id_type=MESH)
        return carry

    lax.fori_loop(1, 8, greet_z, 0)

    def greet_rows(k, carry):
        @pl.when(jnp.logical_or(k != a, a != c))
        def _():
            pl.semaphore_signal(barrier, inc=1, device_id=(k, a), device_id_type=MESH)
        return carry

    lax.fori_loop(0, 16, greet_rows, 0)

    def remote(src, dst, send, recv, device):
        return pltpu.make_async_remote_copy(src_ref=src, dst_ref=dst, send_sem=send, recv_sem=recv,
                                            device_id=device, device_id_type=MESH)

    def wait_bytes(ref, sem):
        pltpu.make_async_copy(ref, ref, sem).wait()

    pending = []

    def later(ref, sem, condition=None):
        pending.append((ref, sem, condition))

    def later_home(inside, outside, sem):
        later(inside, sem, home)
        later(outside, sem, jnp.logical_not(home))

    def wait_home(inside, outside, sem):
        pl.when(home)(functools.partial(wait_bytes, inside, sem))
        pl.when(jnp.logical_not(home))(functools.partial(wait_bytes, outside, sem))

    def drain():
        for ref, sem, condition in pending:
            if condition is None:
                wait_bytes(ref, sem)
            else:
                pl.when(condition)(functools.partial(wait_bytes, ref, sem))

    loads[1].wait()
    row = lax.broadcasted_iota(jnp.int32, (128, 128), 0)
    col = lax.broadcasted_iota(jnp.int32, (128, 128), 1)
    lead = lax.broadcasted_iota(jnp.int32, (1, 128), 1)
    filt = taps_v[...] + jnp.where(lead == 0, 1.0, 0.0)
    rolled = jnp.broadcast_to(filt, (128, 128))
    for bit in range(7):
        rolled = jnp.where((row // (1 << bit)) % 2 == 1, pltpu.roll(rolled, 1 << bit, 1), rolled)
    first = jnp.where(col >= row, rolled, 0.0)
    second = jnp.where(col < row, rolled, 0.0)
    high, low = split(jnp.concatenate([second, first], axis=0))
    w_high[...] = high
    w_low[...] = low
    high, low = split(jnp.concatenate([second.T, first.T], axis=1))
    filter_t[...] = jnp.concatenate([high, low], axis=0)

    loads[0].wait()
    @pl.when(a == c)
    def _():
        pl.semaphore_wait(barrier, 52)

    @pl.when(a != c)
    def _():
        pl.semaphore_wait(barrier, 53)

    def along_y(p, m, i):
        for ky in (1, 3, 2):
            target = ((y + ky) % 4) * 4 + ma
            remote(gather.at[p, m, y], gather.at[p, m, y], ag_send.at[p], ag_recv.at[p, i * 4 + ky], (target, c)).start()

    def gather_arc(p):
        own = gather.at[p, ma, y]
        remote(own, own, ag_send.at[p], ag_recv.at[p, 4], (y * 4 + (ma + 2) % 4, c)).start()
        along_y(p, ma, 0)
        remote(own, own, fwd_send.at[p], fwd_recv.at[p, 0], (sibling, c)).start()
        later(landed.at[0:2, 0:7], ag_send.at[p])

    def forward(p):
        wait_bytes(gather.at[p, (ma + 2) % 4, y], ag_recv.at[p, 4])
        along_y(p, (ma + 2) % 4, 1)

        def block_of(s):
            return ((xlo + s // 2) % 2) * 2 + (core + s % 2) % 2

        def finish(s):
            m = block_of(s)
            wait_bytes(pair_part.at[p, m], part_recv.at[p, m])
            for h in range(2):
                at = 2 * xh + h
                partial[p, m, at] = partial[p, m, at] + pair_part[p, m, h]

                @pl.when(4 * h + m != z)
                def _():
                    remote(partial.at[p, m, at], landed.at[p, (4 * h + m + 8 - z) % 8], rs_send.at[p], rs_recv.at[p],
                           (a, xh * 8 + 4 * h + m)).start()

        def step(s, carry):
            i, j = s // 2, s % 2
            m = block_of(s)

            @pl.when(j == 0)
            def _():
                for ky in range(4):
                    block = gather.at[p, m, (y + 4 - ky) % 4]
                    if ky == 0:
                        @pl.when(i > 0)
                        def _():
                            remote(block, block, fwd_send.at[p], fwd_recv.at[p, i], (sibling, c)).start()
                    else:
                        wait_bytes(block, ag_recv.at[p, i * 4 + ky])
                        remote(block, block, fwd_send.at[p], fwd_recv.at[p, i], (sibling, c)).start()

            @pl.when(j == 1)
            def _():
                wait_bytes(gather.at[p, m], fwd_recv.at[p, i])

            product = dot3(gather[p, m].reshape(64, 1024), t_high[...], t_low[...])
            partial[p, m] = product.reshape(4, 16, 512)
            remote(partial.at[p, m, pl.ds(2 - 2 * xh, 2)], pair_part.at[p, m], part_send.at[p], part_recv.at[p, m], (a, across)).start()

            @pl.when(s >= 2)
            def _():
                finish(s - 2)
            return carry

        lax.fori_loop(0, 4, step, 0)
        finish(2)
        finish(3)
        later(gather.at[p, 0:2], fwd_send.at[p])
        later(pair_part.at[p], part_send.at[p])
        later(landed.at[p, 1:8], rs_send.at[p])

    def forward_sum(p):
        wait_bytes(landed.at[p, 1:8], rs_recv.at[p])
        total = partial[p, mc, yc]
        for k in range(1, 8):
            total = total + landed[p, k]
        return total

    def gather_coef(it, value):
        own_rows[it] = value
        own, there = own_rows.at[it], back_rows.at[it, xlc, core, yc]

        @pl.when(home)
        def _():
            there[...] = value

        for dz in (4, 3, 5, 2, 6, 1, 7):
            remote(own, there, bg_send.at[it], bg_recv.at[it, dz, core], (a - core + side, xh * 8 + (z + dz) % 8)).start()

        @pl.when(jnp.logical_not(home))
        def _():
            remote(own, there, bg_send.at[it], bg_recv.at[it, 0, core], (sibling, c)).start()

        later_home(landed.at[it, 1:8], landed.at[it], bg_send.at[it])

    def gather_coef_on(it):
        odd = (core + side) % 2
        for n in (0, 2, 1, 3):
            for t in (0, 1):
                dz = 2 * n + odd
                source = (z + 8 - dz) % 8
                block = back_rows.at[it, (source % 4) // 2, (core + t) % 2, 2 * xh + source // 4]
                arrived = functools.partial(wait_bytes, block, bg_recv.at[it, dz, (core + t) % 2])
                if n == 0 and t == 0:
                    pl.when(odd == 1)(arrived)
                else:
                    arrived()
                remote(block, block, bf_send.at[it], bf_recv.at[it], (a, across)).start()
        wait_bytes(back_rows.at[it, 0], bf_recv.at[it])
        later(back_rows.at[it, 0], bf_send.at[it])

    def spread(it, one, two):
        @pl.when(home)
        def _():
            own = vector.at[it, xlc, yc]
            own[...] = pack(one, two)

            def step(k, carry):
                remote(own, own, vec_send.at[it], vec_recv.at[it], (a, (c + k) % 16)).start()
                return carry

            lax.fori_loop(1, 16, step, 0)
        later(sum_dst.at[it, 1:16], vec_send.at[it], home)

    def spread_wait(it):
        wait_home(sum_dst.at[it, 1:8], sum_dst.at[it, 0:8], vec_recv.at[it])

    def spread_rows(it, xl, which):
        return jnp.concatenate([unpack(vector[it, xl, k], which) for k in range(4)], axis=0)

    def weighted_rows(it, xl, half):
        rows = back_rows[0, xl, half].reshape(64, 512)
        if it == 0:
            return rows * lax.rsqrt(1.0 + rows * rows * spread_rows(0, xl, 0))
        rows = rows - spread_rows(1, xl, 0) * back_rows[1, xl, half].reshape(64, 512)
        return rows * lax.rsqrt(1.0 + rows * rows * spread_rows(1, xl, 1))

    def backward(it):
        for i in (1, 0):
            xl = (xlo + i) % 2
            product = dot3(weighted_rows(it, xl, 0), g_high[0], g_low[0])
            product = product + dot3(weighted_rows(it, xl, 1), g_high[1], g_low[1])
            grad_part[it, xl] = product.reshape(4, 16, 1024)
            for ky in (2, 1, 3, 0):
                if ky == 0 and i == 0:
                    continue
                ty = (y + ky) % 4
                remote(grad_part.at[it, xl, ty], grad_land.at[it, i * 4 + ky], ra_send.at[it], ra_recv.at[it],
                       (ty * 4 + 2 * xl + core, c)).start()
        later(grad_land.at[it, 1:8], ra_send.at[it])

    def backward_sum(it):
        wait_bytes(grad_land.at[it, 1:8], ra_recv.at[it])
        total = grad_part[it, xlo, y]
        for k in range(1, 8):
            total = total + grad_land[it, k]
        return total

    def whiten(n, value):
        edge_src[n] = value[:, 384:512]

        @pl.when(a < 15)
        def _():
            remote(edge_src.at[n], edge_dst.at[n], edge_send.at[n], edge_recv.at[n], (a + 1, c)).start()

        later(edge_src.at[n], edge_send.at[n], a < 15)

        @pl.when(a == 0)
        def _():
            edge_dst[n] = jnp.zeros((16, 128), F32)

        inside = filter_blocks(jnp.concatenate([jnp.zeros((16, 128), F32), value], axis=1))
        inside = unblock(dot3(inside, w_high[...], w_low[...]))

        @pl.when(a > 0)
        def _():
            wait_bytes(edge_dst.at[n], edge_recv.at[n])

        outside = dot3(edge_dst[n], w_high[0:128, :], w_low[0:128, :])
        return jnp.concatenate([inside[:, 0:128] + outside, inside[:, 128:512]], axis=1)

    def time_sum(n, values):
        sum_src[n] = fold([lanes(value) for value in values])

        def step(k, carry):
            remote(sum_src.at[n], sum_dst.at[n, k], sum_send.at[n], sum_recv.at[n], ((a + k) % 16, c)).start()
            return carry

        lax.fori_loop(1, 16, step, 0)
        later(sum_dst.at[n, 1:16], sum_send.at[n])

    def time_sum_wait(n, count):
        wait_bytes(sum_dst.at[n, 1:16], sum_recv.at[n])
        total = sum_src[n]
        for k in range(1, 16):
            total = total + sum_dst[n, k]
        return unfold(total, count)

    def coef_sum(it, product, old):
        gp_src[it] = fold([lanes(product), lanes(old)])

        def step(k, carry):
            remote(gp_src.at[it], gp_dst.at[it, k], gp_send.at[it], gp_recv.at[it], (a, (c + k) % 16)).start()
            return carry

        lax.fori_loop(1, 16, step, 0)
        later(gp_dst.at[it, 1:16], gp_send.at[it])

    def coef_sum_wait(it):
        wait_bytes(gp_dst.at[it, 1:16], gp_recv.at[it])
        total = gp_src[it]
        for k in range(1, 16):
            total = total + gp_dst[it, k]

        @pl.when(a == c)
        def _():
            diag_gp[it] = total

            def step(k, carry):
                remote(diag_gp.at[it], diag_gp.at[it], diag_send.at[it], diag_recv.at[it], ((a + k) % 16, c)).start()
                return carry

            lax.fori_loop(1, 16, step, 0)
        later(gp_dst.at[it, 1:16], diag_send.at[it], a == c)
        return unfold(total, 2)

    def diag_gp_wait(it):
        @pl.when(a != c)
        def _():
            wait_bytes(diag_gp.at[it], diag_recv.at[it])
        return unfold(diag_gp[it], 2)

    def time_sum_rows():
        @pl.when(a == c)
        def _():
            cur_dst[a] = sum_src[ITERS]

        def step(k, carry):
            @pl.when(jnp.logical_or(c != a, k != c))
            def _():
                remote(sum_src.at[ITERS], cur_dst.at[a], cur_send, cur_recv, (c, k)).start()
            return carry

        lax.fori_loop(0, 16, step, 0)
        later(cur_dst.at[0:15], cur_send, a == c)
        later(cur_dst, cur_send, a != c)

    def time_sum_rows_wait():
        pl.when(a == c)(functools.partial(wait_bytes, cur_dst.at[0:15], cur_recv))
        pl.when(a != c)(functools.partial(wait_bytes, cur_dst, cur_recv))
        total = cur_dst[0]
        for k in range(1, 16):
            total = total + cur_dst[k]
        return unfold(total, 1)

    gather_arc(0)
    loads[2].wait()

    @pl.when(a < 15)
    def _():
        remote(design_f.at[384:512], halo, halo_sem.at[0], halo_sem.at[1], (a + 1, c)).start()

    later(halo, halo_sem.at[0], a < 15)

    @pl.when(a == 0)
    def _():
        halo[...] = jnp.zeros((128, 1024), F32)

    def prepare(r, carry):
        at = pl.ds(pl.multiple_of(r * 128, 128), 128)
        piece = design_f[at, :]
        high, low = split(piece)
        d_high[pl.ds(pl.multiple_of(r * 128 + 128, 128), 128), :] = high
        d_low[pl.ds(pl.multiple_of(r * 128 + 128, 128), 128), :] = low
        high, low = split(piece.T)
        t_high[:, at] = high
        t_low[:, at] = low
        return carry

    lax.fori_loop(0, 4, prepare, 0)
    forward(0)

    @pl.when(a > 0)
    def _():
        wait_bytes(halo, halo_sem.at[1])

    high, low = split(halo[...])
    d_high[0:128, :] = high
    d_low[0:128, :] = low

    def whiten_design(r, carry):
        at = pl.ds(pl.multiple_of(r * 128, 128), 256)
        both = jnp.dot(filter_t[...], d_high[at, :], preferred_element_type=F32)
        rest = jnp.dot(filter_t[0:128, :], d_low[at, :], preferred_element_type=F32)
        value = both[0:128] + both[128:256] + rest
        at = pl.ds(pl.multiple_of(r * 128, 128), 128)
        g_f[at, :] = value
        high, low = split(value)
        g_high[core, at, :] = high
        g_low[core, at, :] = low
        return carry

    lax.fori_loop(0, 4, whiten_design, 0)
    remote(g_f, g_s, design_sem.at[0], design_sem.at[1], (sibling, c)).start()
    later(g_f, design_sem.at[0])
    wait_bytes(g_s, design_sem.at[1])

    def split_sibling(r, carry):
        at = pl.ds(pl.multiple_of(r * 128, 128), 128)
        high, low = split(g_s[at, :])
        g_high[1 - core, at, :] = high
        g_low[1 - core, at, :] = low
        return carry

    lax.fori_loop(0, 4, split_sibling, 0)
    loads[3].wait()
    loads[4].wait()
    residual = obs_v[...] - forward_sum(0)
    whitened = whiten(0, residual)
    time_sum(0, [whitened * whitened])
    gather_coef(0, whitened)
    square, = time_sum_wait(0, 1)
    factor = 1.0 / (square * (HUBER_SQUARE / TOTAL_OBS) + EPSILON)
    spread(0, factor, factor)

    for it in range(ITERS):
        weights = lax.rsqrt(1.0 + whitened * whitened * factor)
        gather_coef_on(it)
        spread_wait(it)
        backward(it)
        gradient = backward_sum(it)
        conditioned = precond_v[...] * gradient
        gather[it + 1, ma, y] = conditioned
        gather_arc(it + 1)
        if it == 0:
            coef_sum(it, gradient * conditioned, gradient)
        else:
            coef_sum(it, gradient * conditioned, gradient * direction)
        forward(it + 1)
        gp_a, go_a = coef_sum_wait(it)
        if it == 0:
            first_direction = direction = conditioned
        else:
            beta = gp_a / gp_a_old
            direction = conditioned + beta * direction
            grad_dir = gp_a + beta * go_a
        image = forward_sum(it + 1)
        imaged = whiten(it + 1, image)
        gp_c, go_c = diag_gp_wait(it)
        if it == 0:
            time_sum(1, [weights * imaged * imaged, whitened * imaged, imaged * imaged])
            gather_coef(1, imaged)
            curvature, cross, own = time_sum_wait(1, 3)
            alpha = gp_c / curvature
            square = jnp.maximum(square - 2.0 * alpha * cross + alpha * alpha * own, 0.0)
            factor = 1.0 / (square * (HUBER_SQUARE / TOTAL_OBS) + EPSILON)
            spread(1, alpha, factor)
            whitened = whitened - alpha * imaged
            gp_a_old, gp_c_old, image_old, imaged_old = gp_a, gp_c, image, imaged
        else:
            beta = gp_c / gp_c_old
            image = image + beta * image_old
            imaged = imaged + beta * imaged_old
            time_sum(2, [weights * imaged * imaged])
            time_sum_rows()
            curvature, = time_sum_wait(2, 1)
            alpha = (gp_c + beta * go_c) / curvature
        residual = residual - alpha * image
    misfit_ref[...] = residual
    coefs = gather[0, ma, y] + unpack(vector[1, xlo, y], 0) * first_direction
    curvature, = time_sum_rows_wait()
    coefs_ref[...] = coefs + (grad_dir / curvature) * direction
    drain()


def body(design, observations, start_coefs, precond, taps):
    vmem = pl.BlockSpec(memory_space=pltpu.VMEM)
    dma = pltpu.SemaphoreType.DMA
    scratch = [
        pltpu.VMEM((512, 1024), F32),
        pltpu.VMEM((16, 512), F32), pltpu.VMEM((1, 1024), F32), pltpu.VMEM((1, 128), F32),
        pltpu.VMEM((128, 1024), F32),
        pltpu.VMEM((640, 1024), BF16), pltpu.VMEM((640, 1024), BF16),
        pltpu.VMEM((512, 1024), F32), pltpu.VMEM((512, 1024), F32),
        pltpu.VMEM((2, 512, 1024), BF16), pltpu.VMEM((2, 512, 1024), BF16),
        pltpu.VMEM((1024, 512), BF16), pltpu.VMEM((1024, 512), BF16),
        pltpu.VMEM((256, 128), BF16), pltpu.VMEM((256, 128), BF16), pltpu.VMEM((256, 256), BF16),
        pltpu.VMEM((3, 4, 4, 16, 1024), F32),
        pltpu.VMEM((3, 4, 4, 16, 512), F32),
        pltpu.VMEM((3, 4, 2, 16, 512), F32),
        pltpu.VMEM((3, 8, 16, 512), F32),
        pltpu.VMEM((2, 16, 512), F32),
        pltpu.VMEM((2, 2, 2, 4, 16, 512), F32),
        pltpu.VMEM((2, 2, 4, 16, 1024), F32),
        pltpu.VMEM((2, 8, 16, 1024), F32),
        pltpu.VMEM((3, 16, 128), F32), pltpu.VMEM((3, 16, 128), F32),
        pltpu.VMEM((3, 8, 128), F32), pltpu.VMEM((3, 16, 8, 128), F32),
        pltpu.VMEM((2, 8, 128), F32), pltpu.VMEM((2, 16, 8, 128), F32),
        pltpu.VMEM((2, 8, 128), F32), pltpu.VMEM((16, 8, 128), F32),
        pltpu.VMEM((2, 2, 4, 8, 128), F32),
        dma((5,)), dma((2,)), dma((2,)), dma, dma,
        dma((3,)), dma((3, 8)), dma((3,)), dma((3, 2)), dma((3,)), dma((3, 4)), dma((3,)), dma((3,)),
        dma((2,)), dma((2, 8, 2)), dma((2,)), dma((2,)), dma((2,)), dma((2,)),
        dma((3,)), dma((3,)), dma((3,)), dma((3,)), dma((2,)), dma((2,)), dma((2,)), dma((2,)), dma((2,)), dma((2,)),
    ]
    return pl.pallas_call(
        kernel,
        out_shape=(jax.ShapeDtypeStruct(start_coefs.shape, F32), jax.ShapeDtypeStruct(observations.shape, F32)),
        in_specs=[pl.BlockSpec(memory_space=pltpu.HBM)] * 5,
        out_specs=(vmem, vmem),
        scratch_shapes=scratch,
        compiler_params=pltpu.CompilerParams(collective_id=0, has_side_effects=True, vmem_limit_bytes=60 << 20),
    )(design, observations, start_coefs, precond.reshape(1, -1), taps.reshape(1, -1))


def solution(mesh):
    placed = (P("arc", "coef"), P("coef", "arc"), P("arc", "coef"), P("coef"), P())
    return jax.shard_map(
        body,
        mesh=mesh,
        in_specs=placed,
        out_specs=(P("arc", "coef"), P("coef", "arc")),
        check_vma=False,
    )
```

```python
import functools
import jax
import jax.numpy as jnp
from jax import lax
from jax.experimental import pallas as pl
from jax.experimental.pallas import tpu as pltpu
from jax.sharding import PartitionSpec as P

ITERS = 2
TOTAL_OBS = 8192
HUBER_SQUARE = 2.25
EPSILON = 1e-06

F32 = jnp.float32
BF16 = jnp.bfloat16
MESH = pl.DeviceIdType.MESH


def split(value):
    high = value.astype(BF16)
    low = (value - high.astype(F32)).astype(BF16)
    return high, low


def dot3(value, weight_high, weight_low):
    rows = value.shape[0]
    high, low = split(value)
    both = jnp.dot(jnp.concatenate([high, low], axis=0), weight_high, preferred_element_type=F32)
    rest = jnp.dot(high, weight_low, preferred_element_type=F32)
    return both[:rows] + both[rows:] + rest


def lanes(value):
    total = value[:, 0:128]
    for start in range(128, value.shape[1], 128):
        total = total + value[:, start:start + 128]
    return total


def fold(values):
    group = lax.broadcasted_iota(jnp.int32, (8, 128), 1) // 16
    tile = jnp.zeros((8, 128), F32)
    for n, value in enumerate(values):
        for shift in (64, 32, 16):
            value = value + pltpu.roll(value, shift, 1)
        tile = jnp.where(group == 2 * n, value[0:8], tile)
        tile = jnp.where(group == 2 * n + 1, value[8:16], tile)
    return tile


def unfold(tile, count):
    for shift in (8, 4, 2, 1):
        tile = tile + pltpu.roll(tile, shift, 1)
    return [jnp.concatenate([tile[:, 32 * n + 15:32 * n + 16], tile[:, 32 * n + 31:32 * n + 32]], axis=0) for n in range(count)]


def pack(one, two):
    lane = lax.broadcasted_iota(jnp.int32, (8, 128), 1)
    return jnp.where(lane < 64, jnp.where(lane < 32, one[0:8], one[8:16]), jnp.where(lane < 96, two[0:8], two[8:16]))


def unpack(tile, which):
    start = 64 * which
    return jnp.concatenate([tile[:, start:start + 1], tile[:, start + 32:start + 33]], axis=0)


def filter_blocks(extended):
    return jnp.concatenate([extended[:, j * 128:(j + 2) * 128] for j in range(4)], axis=0)


def unblock(value):
    return jnp.concatenate([value[j * 16:(j + 1) * 16] for j in range(4)], axis=1)


def kernel(design_hbm, obs_hbm, start_hbm, precond_hbm, taps_hbm, coefs_ref, misfit_ref,
           design_f, obs_v, precond_v, taps_v, halo, d_high, d_low, g_f, g_s, g_high, g_low, t_high, t_low, w_high, w_low, filter_t,
           gather, partial, pair_part, landed, own_rows, back_rows, grad_part, grad_land,
           edge_src, edge_dst, sum_src, sum_dst, gp_src, gp_dst, diag_gp, cur_dst, vector,
           load_sem, halo_sem, design_sem, cur_send, cur_recv, ag_send, ag_recv, fwd_send, fwd_recv, part_send, part_recv, rs_send, rs_recv,
           bg_send, bg_recv, bf_send, bf_recv, ra_send, ra_recv,
           edge_send, edge_recv, sum_send, sum_recv, gp_send, gp_recv, diag_send, diag_recv, vec_send, vec_recv):
    a = lax.axis_index("arc")
    c = lax.axis_index("coef")
    y, ma = a // 4, a % 4
    xlo, core = ma // 2, ma % 2
    xh, z = c // 8, c % 8
    yc, mc = c // 4, c % 4
    xlc, side = mc // 2, mc % 2
    sibling = a + 1 - 2 * core
    home = core == side
    across = (xh * 8 + 8) % 16 + z

    loads = []
    for n, (source, target) in enumerate([(start_hbm, gather.at[0, ma, y]), (taps_hbm, taps_v), (design_hbm, design_f),
                                          (obs_hbm, obs_v), (precond_hbm, precond_v)]):
        loads.append(pltpu.make_async_copy(source, target, load_sem.at[n]))
        loads[-1].start()

    barrier = pltpu.get_barrier_semaphore()

    def greet(k, carry):
        pl.semaphore_signal(barrier, inc=1, device_id=((a + k) % 16, c), device_id_type=MESH)
        pl.semaphore_signal(barrier, inc=1, device_id=(a, (c + k) % 16), device_id_type=MESH)
        return carry

    lax.fori_loop(1, 16, greet, 0)

    def greet_z(k, carry):
        pl.semaphore_signal(barrier, inc=1, device_id=(sibling, xh * 8 + (z + k) % 8), device_id_type=MESH)
        return carry

    lax.fori_loop(1, 8, greet_z, 0)

    def greet_rows(k, carry):
        @pl.when(jnp.logical_or(k != a, a != c))
        def _():
            pl.semaphore_signal(barrier, inc=1, device_id=(k, a), device_id_type=MESH)
        return carry

    lax.fori_loop(0, 16, greet_rows, 0)

    def remote(src, dst, send, recv, device):
        return pltpu.make_async_remote_copy(src_ref=src, dst_ref=dst, send_sem=send, recv_sem=recv,
                                            device_id=device, device_id_type=MESH)

    def wait_bytes(ref, sem):
        pltpu.make_async_copy(ref, ref, sem).wait()

    pending = []

    def later(ref, sem, condition=None):
        pending.append((ref, sem, condition))

    def later_home(inside, outside, sem):
        later(inside, sem, home)
        later(outside, sem, jnp.logical_not(home))

    def wait_home(inside, outside, sem):
        pl.when(home)(functools.partial(wait_bytes, inside, sem))
        pl.when(jnp.logical_not(home))(functools.partial(wait_bytes, outside, sem))

    def drain():
        for ref, sem, condition in pending:
            if condition is None:
                wait_bytes(ref, sem)
            else:
                pl.when(condition)(functools.partial(wait_bytes, ref, sem))

    loads[1].wait()
    row = lax.broadcasted_iota(jnp.int32, (128, 128), 0)
    col = lax.broadcasted_iota(jnp.int32, (128, 128), 1)
    lead = lax.broadcasted_iota(jnp.int32, (1, 128), 1)
    filt = taps_v[...] + jnp.where(lead == 0, 1.0, 0.0)
    rolled = jnp.broadcast_to(filt, (128, 128))
    for bit in range(7):
        rolled = jnp.where((row // (1 << bit)) % 2 == 1, pltpu.roll(rolled, 1 << bit, 1), rolled)
    first = jnp.where(col >= row, rolled, 0.0)
    second = jnp.where(col < row, rolled, 0.0)
    high, low = split(jnp.concatenate([second, first], axis=0))
    w_high[...] = high
    w_low[...] = low
    high, low = split(jnp.concatenate([second.T, first.T], axis=1))
    filter_t[...] = jnp.concatenate([high, low], axis=0)

    loads[0].wait()
    @pl.when(a == c)
    def _():
        pl.semaphore_wait(barrier, 52)

    @pl.when(a != c)
    def _():
        pl.semaphore_wait(barrier, 53)

    def along_y(p, m, i):
        for ky in (1, 3, 2):
            target = ((y + ky) % 4) * 4 + ma
            remote(gather.at[p, m, y], gather.at[p, m, y], ag_send.at[p], ag_recv.at[p, i * 4 + ky], (target, c)).start()

    def gather_arc(p):
        own = gather.at[p, ma, y]
        remote(own, own, ag_send.at[p], ag_recv.at[p, 4], (y * 4 + (ma + 2) % 4, c)).start()
        along_y(p, ma, 0)
        remote(own, own, fwd_send.at[p], fwd_recv.at[p, 0], (sibling, c)).start()
        later(landed.at[0:2, 0:7], ag_send.at[p])

    def forward(p):
        wait_bytes(gather.at[p, (ma + 2) % 4, y], ag_recv.at[p, 4])
        along_y(p, (ma + 2) % 4, 1)

        def block_of(s):
            return ((xlo + s // 2) % 2) * 2 + (core + s % 2) % 2

        def finish(s):
            m = block_of(s)
            wait_bytes(pair_part.at[p, m], part_recv.at[p, m])
            for h in range(2):
                at = 2 * xh + h
                partial[p, m, at] = partial[p, m, at] + pair_part[p, m, h]

                @pl.when(4 * h + m != z)
                def _():
                    remote(partial.at[p, m, at], landed.at[p, (4 * h + m + 8 - z) % 8], rs_send.at[p], rs_recv.at[p],
                           (a, xh * 8 + 4 * h + m)).start()

        def step(s, carry):
            i, j = s // 2, s % 2
            m = block_of(s)

            @pl.when(j == 0)
            def _():
                for ky in range(4):
                    block = gather.at[p, m, (y + 4 - ky) % 4]
                    if ky == 0:
                        @pl.when(i > 0)
                        def _():
                            remote(block, block, fwd_send.at[p], fwd_recv.at[p, i], (sibling, c)).start()
                    else:
                        wait_bytes(block, ag_recv.at[p, i * 4 + ky])
                        remote(block, block, fwd_send.at[p], fwd_recv.at[p, i], (sibling, c)).start()

            @pl.when(j == 1)
            def _():
                wait_bytes(gather.at[p, m], fwd_recv.at[p, i])

            product = dot3(gather[p, m].reshape(64, 1024), t_high[...], t_low[...])
            partial[p, m] = product.reshape(4, 16, 512)
            remote(partial.at[p, m, pl.ds(2 - 2 * xh, 2)], pair_part.at[p, m], part_send.at[p], part_recv.at[p, m], (a, across)).start()

            @pl.when(s >= 2)
            def _():
                finish(s - 2)
            return carry

        lax.fori_loop(0, 4, step, 0)
        finish(2)
        finish(3)
        later(gather.at[p, 0:2], fwd_send.at[p])
        later(pair_part.at[p], part_send.at[p])
        later(landed.at[p, 1:8], rs_send.at[p])

    def forward_sum(p):
        wait_bytes(landed.at[p, 1:8], rs_recv.at[p])
        total = partial[p, mc, yc]
        for k in range(1, 8):
            total = total + landed[p, k]
        return total

    def columns(part):
        return pl.ds(0, 128) if part else pl.ds(128, 384)

    def gather_coef(it, part, value):
        at = columns(part)
        own, there = own_rows.at[it, :, at], back_rows.at[it, xlc, core, yc, :, at]
        own[...] = value

        @pl.when(home)
        def _():
            there[...] = value

        for dz in (4, 3, 5, 2, 6, 1, 7):
            remote(own, there, bg_send.at[it], bg_recv.at[it, part, dz, core],
                   (a - core + side, xh * 8 + (z + dz) % 8)).start()

        @pl.when(jnp.logical_not(home))
        def _():
            remote(own, there, bg_send.at[it], bg_recv.at[it, part, 0, core], (sibling, c)).start()

        if part == 1:
            later_home(landed.at[it, 1:8], landed.at[it], bg_send.at[it])

    def gather_coef_on(it):
        odd = (core + side) % 2
        for part in (0, 1):
            for n in (0, 2, 1, 3):
                for t in (0, 1):
                    dz = 2 * n + odd
                    source = (z + 8 - dz) % 8
                    block = back_rows.at[it, (source % 4) // 2, (core + t) % 2, 2 * xh + source // 4, :, columns(part)]
                    arrived = functools.partial(wait_bytes, block, bg_recv.at[it, part, dz, (core + t) % 2])
                    if n == 0 and t == 0:
                        pl.when(odd == 1)(arrived)
                    else:
                        arrived()
                    remote(block, block, bf_send.at[it], bf_recv.at[it], (a, across)).start()
        wait_bytes(back_rows.at[it, 0], bf_recv.at[it])
        later(back_rows.at[it, 0], bf_send.at[it])

    def spread(it, one, two):
        @pl.when(home)
        def _():
            own = vector.at[it, xlc, yc]
            own[...] = pack(one, two)

            def step(k, carry):
                remote(own, own, vec_send.at[it], vec_recv.at[it], (a, (c + k) % 16)).start()
                return carry

            lax.fori_loop(1, 16, step, 0)
        later(sum_dst.at[it, 1:16], vec_send.at[it], home)

    def spread_wait(it):
        wait_home(sum_dst.at[it, 1:8], sum_dst.at[it, 0:8], vec_recv.at[it])

    def spread_rows(it, xl, which):
        return jnp.concatenate([unpack(vector[it, xl, k], which) for k in range(4)], axis=0)

    def weighted_rows(it, xl, half):
        rows = back_rows[0, xl, half].reshape(64, 512)
        if it == 0:
            return rows * lax.rsqrt(1.0 + rows * rows * spread_rows(0, xl, 0))
        rows = rows - spread_rows(1, xl, 0) * back_rows[1, xl, half].reshape(64, 512)
        return rows * lax.rsqrt(1.0 + rows * rows * spread_rows(1, xl, 1))

    def backward(it):
        for i in (1, 0):
            xl = (xlo + i) % 2
            product = dot3(weighted_rows(it, xl, 0), g_high[0], g_low[0])
            product = product + dot3(weighted_rows(it, xl, 1), g_high[1], g_low[1])
            grad_part[it, xl] = product.reshape(4, 16, 1024)
            for ky in (2, 1, 3, 0):
                if ky == 0 and i == 0:
                    continue
                ty = (y + ky) % 4
                remote(grad_part.at[it, xl, ty], grad_land.at[it, i * 4 + ky], ra_send.at[it], ra_recv.at[it],
                       (ty * 4 + 2 * xl + core, c)).start()
        later(grad_land.at[it, 1:8], ra_send.at[it])

    def backward_sum(it):
        wait_bytes(grad_land.at[it, 1:8], ra_recv.at[it])
        total = grad_part[it, xlo, y]
        for k in range(1, 8):
            total = total + grad_land[it, k]
        return total

    def whiten(n, value, ahead=None):
        edge_src[n] = value[:, 384:512]

        @pl.when(a < 15)
        def _():
            remote(edge_src.at[n], edge_dst.at[n], edge_send.at[n], edge_recv.at[n], (a + 1, c)).start()

        later(edge_src.at[n], edge_send.at[n], a < 15)

        @pl.when(a == 0)
        def _():
            edge_dst[n] = jnp.zeros((16, 128), F32)

        inside = filter_blocks(jnp.concatenate([jnp.zeros((16, 128), F32), value], axis=1))
        inside = unblock(dot3(inside, w_high[...], w_low[...]))
        if ahead is not None:
            ahead(inside[:, 128:512])

        @pl.when(a > 0)
        def _():
            wait_bytes(edge_dst.at[n], edge_recv.at[n])

        outside = dot3(edge_dst[n], w_high[0:128, :], w_low[0:128, :])
        return jnp.concatenate([inside[:, 0:128] + outside, inside[:, 128:512]], axis=1)

    def time_sum(n, values):
        sum_src[n] = fold([lanes(value) for value in values])

        def step(k, carry):
            remote(sum_src.at[n], sum_dst.at[n, k], sum_send.at[n], sum_recv.at[n], ((a + k) % 16, c)).start()
            return carry

        lax.fori_loop(1, 16, step, 0)
        later(sum_dst.at[n, 1:16], sum_send.at[n])

    def time_sum_wait(n, count):
        wait_bytes(sum_dst.at[n, 1:16], sum_recv.at[n])
        total = sum_src[n]
        for k in range(1, 16):
            total = total + sum_dst[n, k]
        return unfold(total, count)

    def coef_sum(it, product, old):
        gp_src[it] = fold([lanes(product), lanes(old)])

        def step(k, carry):
            remote(gp_src.at[it], gp_dst.at[it, k], gp_send.at[it], gp_recv.at[it], (a, (c + k) % 16)).start()
            return carry

        lax.fori_loop(1, 16, step, 0)
        later(gp_dst.at[it, 1:16], gp_send.at[it])

    def coef_sum_wait(it):
        wait_bytes(gp_dst.at[it, 1:16], gp_recv.at[it])
        total = gp_src[it]
        for k in range(1, 16):
            total = total + gp_dst[it, k]

        @pl.when(a == c)
        def _():
            diag_gp[it] = total

            def step(k, carry):
                remote(diag_gp.at[it], diag_gp.at[it], diag_send.at[it], diag_recv.at[it], ((a + k) % 16, c)).start()
                return carry

            lax.fori_loop(1, 16, step, 0)
        later(gp_dst.at[it, 1:16], diag_send.at[it], a == c)
        return unfold(total, 2)

    def diag_gp_wait(it):
        @pl.when(a != c)
        def _():
            wait_bytes(diag_gp.at[it], diag_recv.at[it])
        return unfold(diag_gp[it], 2)

    def time_sum_rows():
        @pl.when(a == c)
        def _():
            cur_dst[a] = sum_src[ITERS]

        def step(k, carry):
            @pl.when(jnp.logical_or(c != a, k != c))
            def _():
                remote(sum_src.at[ITERS], cur_dst.at[a], cur_send, cur_recv, (c, k)).start()
            return carry

        lax.fori_loop(0, 16, step, 0)
        later(cur_dst.at[0:15], cur_send, a == c)
        later(cur_dst, cur_send, a != c)

    def time_sum_rows_wait():
        pl.when(a == c)(functools.partial(wait_bytes, cur_dst.at[0:15], cur_recv))
        pl.when(a != c)(functools.partial(wait_bytes, cur_dst, cur_recv))
        total = cur_dst[0]
        for k in range(1, 16):
            total = total + cur_dst[k]
        return unfold(total, 1)

    gather_arc(0)
    loads[2].wait()

    def prepare(r, carry):
        at = pl.ds(pl.multiple_of(r * 128, 128), 128)
        piece = design_f[at, :]
        high, low = split(piece)
        d_high[pl.ds(pl.multiple_of(r * 128 + 128, 128), 128), :] = high
        d_low[pl.ds(pl.multiple_of(r * 128 + 128, 128), 128), :] = low
        high, low = split(piece.T)
        t_high[:, at] = high
        t_low[:, at] = low
        return carry

    lax.fori_loop(0, 4, prepare, 0)
    forward(0)

    @pl.when(a < 15)
    def _():
        remote(design_f.at[384:512], halo, halo_sem.at[0], halo_sem.at[1], (a + 1, c)).start()

    later(halo, halo_sem.at[0], a < 15)

    @pl.when(a == 0)
    def _():
        halo[...] = jnp.zeros((128, 1024), F32)


    loads[3].wait()
    loads[4].wait()
    residual = obs_v[...] - forward_sum(0)
    whitened = whiten(0, residual, functools.partial(gather_coef, 0, 0))
    time_sum(0, [whitened * whitened])
    gather_coef(0, 1, whitened[:, 0:128])

    @pl.when(a > 0)
    def _():
        wait_bytes(halo, halo_sem.at[1])

    high, low = split(halo[...])
    d_high[0:128, :] = high
    d_low[0:128, :] = low

    def whiten_design(r, carry):
        at = pl.ds(pl.multiple_of(r * 128, 128), 256)
        both = jnp.dot(filter_t[...], d_high[at, :], preferred_element_type=F32)
        rest = jnp.dot(filter_t[0:128, :], d_low[at, :], preferred_element_type=F32)
        value = both[0:128] + both[128:256] + rest
        at = pl.ds(pl.multiple_of(r * 128, 128), 128)
        g_f[at, :] = value
        high, low = split(value)
        g_high[core, at, :] = high
        g_low[core, at, :] = low
        return carry

    lax.fori_loop(0, 4, whiten_design, 0)
    remote(g_f, g_s, design_sem.at[0], design_sem.at[1], (sibling, c)).start()
    later(g_f, design_sem.at[0])

    square, = time_sum_wait(0, 1)
    factor = 1.0 / (square * (HUBER_SQUARE / TOTAL_OBS) + EPSILON)
    spread(0, factor, factor)

    for it in range(ITERS):
        weights = lax.rsqrt(1.0 + whitened * whitened * factor)
        gather_coef_on(it)
        if it == 0:
            wait_bytes(g_s, design_sem.at[1])

            def split_sibling(r, carry):
                at = pl.ds(pl.multiple_of(r * 128, 128), 128)
                high, low = split(g_s[at, :])
                g_high[1 - core, at, :] = high
                g_low[1 - core, at, :] = low
                return carry

            lax.fori_loop(0, 4, split_sibling, 0)
        spread_wait(it)
        backward(it)
        gradient = backward_sum(it)
        conditioned = precond_v[...] * gradient
        gather[it + 1, ma, y] = conditioned
        gather_arc(it + 1)
        if it == 0:
            coef_sum(it, gradient * conditioned, gradient)
        else:
            coef_sum(it, gradient * conditioned, gradient * direction)
        forward(it + 1)
        gp_a, go_a = coef_sum_wait(it)
        if it == 0:
            first_direction = direction = conditioned
        else:
            beta = gp_a / gp_a_old
            direction = conditioned + beta * direction
            grad_dir = gp_a + beta * go_a
        image = forward_sum(it + 1)
        imaged = whiten(it + 1, image, functools.partial(gather_coef, 1, 0) if it == 0 else None)
        gp_c, go_c = diag_gp_wait(it)
        if it == 0:
            time_sum(1, [weights * imaged * imaged, whitened * imaged, imaged * imaged])
            gather_coef(1, 1, imaged[:, 0:128])
            curvature, cross, own = time_sum_wait(1, 3)
            alpha = gp_c / curvature
            square = jnp.maximum(square - 2.0 * alpha * cross + alpha * alpha * own, 0.0)
            factor = 1.0 / (square * (HUBER_SQUARE / TOTAL_OBS) + EPSILON)
            spread(1, alpha, factor)
            whitened = whitened - alpha * imaged
            gp_a_old, gp_c_old, image_old, imaged_old = gp_a, gp_c, image, imaged
        else:
            beta = gp_c / gp_c_old
            image = image + beta * image_old
            imaged = imaged + beta * imaged_old
            time_sum(2, [weights * imaged * imaged])
            time_sum_rows()
            curvature, = time_sum_wait(2, 1)
            alpha = (gp_c + beta * go_c) / curvature
        residual = residual - alpha * image
    misfit_ref[...] = residual
    coefs = gather[0, ma, y] + unpack(vector[1, xlo, y], 0) * first_direction
    curvature, = time_sum_rows_wait()
    coefs_ref[...] = coefs + (grad_dir / curvature) * direction
    drain()


def body(design, observations, start_coefs, precond, taps):
    vmem = pl.BlockSpec(memory_space=pltpu.VMEM)
    dma = pltpu.SemaphoreType.DMA
    scratch = [
        pltpu.VMEM((512, 1024), F32),
        pltpu.VMEM((16, 512), F32), pltpu.VMEM((1, 1024), F32), pltpu.VMEM((1, 128), F32),
        pltpu.VMEM((128, 1024), F32),
        pltpu.VMEM((640, 1024), BF16), pltpu.VMEM((640, 1024), BF16),
        pltpu.VMEM((512, 1024), F32), pltpu.VMEM((512, 1024), F32),
        pltpu.VMEM((2, 512, 1024), BF16), pltpu.VMEM((2, 512, 1024), BF16),
        pltpu.VMEM((1024, 512), BF16), pltpu.VMEM((1024, 512), BF16),
        pltpu.VMEM((256, 128), BF16), pltpu.VMEM((256, 128), BF16), pltpu.VMEM((256, 256), BF16),
        pltpu.VMEM((3, 4, 4, 16, 1024), F32),
        pltpu.VMEM((3, 4, 4, 16, 512), F32),
        pltpu.VMEM((3, 4, 2, 16, 512), F32),
        pltpu.VMEM((3, 8, 16, 512), F32),
        pltpu.VMEM((2, 16, 512), F32),
        pltpu.VMEM((2, 2, 2, 4, 16, 512), F32),
        pltpu.VMEM((2, 2, 4, 16, 1024), F32),
        pltpu.VMEM((2, 8, 16, 1024), F32),
        pltpu.VMEM((3, 16, 128), F32), pltpu.VMEM((3, 16, 128), F32),
        pltpu.VMEM((3, 8, 128), F32), pltpu.VMEM((3, 16, 8, 128), F32),
        pltpu.VMEM((2, 8, 128), F32), pltpu.VMEM((2, 16, 8, 128), F32),
        pltpu.VMEM((2, 8, 128), F32), pltpu.VMEM((16, 8, 128), F32),
        pltpu.VMEM((2, 2, 4, 8, 128), F32),
        dma((5,)), dma((2,)), dma((2,)), dma, dma,
        dma((3,)), dma((3, 8)), dma((3,)), dma((3, 2)), dma((3,)), dma((3, 4)), dma((3,)), dma((3,)),
        dma((2,)), dma((2, 2, 8, 2)), dma((2,)), dma((2,)), dma((2,)), dma((2,)),
        dma((3,)), dma((3,)), dma((3,)), dma((3,)), dma((2,)), dma((2,)), dma((2,)), dma((2,)), dma((2,)), dma((2,)),
    ]
    return pl.pallas_call(
        kernel,
        out_shape=(jax.ShapeDtypeStruct(start_coefs.shape, F32), jax.ShapeDtypeStruct(observations.shape, F32)),
        in_specs=[pl.BlockSpec(memory_space=pltpu.HBM)] * 5,
        out_specs=(vmem, vmem),
        scratch_shapes=scratch,
        compiler_params=pltpu.CompilerParams(collective_id=0, has_side_effects=True, vmem_limit_bytes=60 << 20),
    )(design, observations, start_coefs, precond.reshape(1, -1), taps.reshape(1, -1))


def solution(mesh):
    placed = (P("arc", "coef"), P("coef", "arc"), P("arc", "coef"), P("coef"), P())
    return jax.shard_map(
        body,
        mesh=mesh,
        in_specs=placed,
        out_specs=(P("arc", "coef"), P("coef", "arc")),
        check_vma=False,
    )
```

```python
import functools
import jax
import jax.numpy as jnp
from jax import lax
from jax.experimental import pallas as pl
from jax.experimental.pallas import tpu as pltpu
from jax.sharding import PartitionSpec as P

ITERS = 2
TOTAL_OBS = 8192
HUBER_SQUARE = 2.25
EPSILON = 1e-06

F32 = jnp.float32
BF16 = jnp.bfloat16
MESH = pl.DeviceIdType.MESH


def split(value):
    high = value.astype(BF16)
    low = (value - high.astype(F32)).astype(BF16)
    return high, low


def dot3(value, weight_high, weight_low):
    rows = value.shape[0]
    high, low = split(value)
    both = jnp.dot(jnp.concatenate([high, low], axis=0), weight_high, preferred_element_type=F32)
    rest = jnp.dot(high, weight_low, preferred_element_type=F32)
    return both[:rows] + both[rows:] + rest


def lanes(value):
    total = value[:, 0:128]
    for start in range(128, value.shape[1], 128):
        total = total + value[:, start:start + 128]
    return total


def fold(values):
    group = lax.broadcasted_iota(jnp.int32, (8, 128), 1) // 16
    tile = jnp.zeros((8, 128), F32)
    for n, value in enumerate(values):
        for shift in (64, 32, 16):
            value = value + pltpu.roll(value, shift, 1)
        tile = jnp.where(group == 2 * n, value[0:8], tile)
        tile = jnp.where(group == 2 * n + 1, value[8:16], tile)
    return tile


def unfold(tile, count):
    for shift in (8, 4, 2, 1):
        tile = tile + pltpu.roll(tile, shift, 1)
    return [jnp.concatenate([tile[:, 32 * n + 15:32 * n + 16], tile[:, 32 * n + 31:32 * n + 32]], axis=0) for n in range(count)]


def pack(one, two):
    lane = lax.broadcasted_iota(jnp.int32, (8, 128), 1)
    return jnp.where(lane < 64, jnp.where(lane < 32, one[0:8], one[8:16]), jnp.where(lane < 96, two[0:8], two[8:16]))


def unpack(tile, which):
    start = 64 * which
    return jnp.concatenate([tile[:, start:start + 1], tile[:, start + 32:start + 33]], axis=0)


def filter_blocks(extended):
    return jnp.concatenate([extended[:, j * 128:(j + 2) * 128] for j in range(4)], axis=0)


def unblock(value):
    return jnp.concatenate([value[j * 16:(j + 1) * 16] for j in range(4)], axis=1)


def kernel(design_hbm, obs_hbm, start_hbm, precond_hbm, taps_hbm, out_ref,
           design_f, obs_v, precond_v, taps_v, halo, d_high, d_low, g_f, g_s, g_high, g_low, t_high, t_low, w_high, w_low, filter_t,
           gather, partial, pair_part, landed, own_rows, back_rows, grad_part, grad_land,
           edge_src, edge_dst, sum_src, sum_dst, gp_src, gp_dst, diag_gp, cur_dst, vector,
           load_sem, halo_sem, design_sem, cur_send, cur_recv, ag_send, ag_recv, fwd_send, fwd_recv, part_send, part_recv, rs_send, rs_recv,
           bg_send, bg_recv, bf_send, bf_recv, ra_send, ra_recv,
           edge_send, edge_recv, sum_send, sum_recv, gp_send, gp_recv, diag_send, diag_recv, vec_send, vec_recv):
    a = lax.axis_index("arc")
    c = lax.axis_index("coef")
    y, ma = a // 4, a % 4
    xlo, core = ma // 2, ma % 2
    xh, z = c // 8, c % 8
    yc, mc = c // 4, c % 4
    xlc, side = mc // 2, mc % 2
    sibling = a + 1 - 2 * core
    home = core == side
    across = (xh * 8 + 8) % 16 + z

    loads = []
    for n, (source, target) in enumerate([(start_hbm, gather.at[0, ma, y]), (taps_hbm, taps_v), (design_hbm, design_f),
                                          (obs_hbm, obs_v), (precond_hbm, precond_v)]):
        loads.append(pltpu.make_async_copy(source, target, load_sem.at[n]))
        loads[-1].start()

    barrier = pltpu.get_barrier_semaphore()

    def greet(k, carry):
        pl.semaphore_signal(barrier, inc=1, device_id=((a + k) % 16, c), device_id_type=MESH)
        pl.semaphore_signal(barrier, inc=1, device_id=(a, (c + k) % 16), device_id_type=MESH)
        return carry

    lax.fori_loop(1, 16, greet, 0)

    def greet_z(k, carry):
        pl.semaphore_signal(barrier, inc=1, device_id=(sibling, xh * 8 + (z + k) % 8), device_id_type=MESH)
        return carry

    lax.fori_loop(1, 8, greet_z, 0)

    def greet_rows(k, carry):
        @pl.when(jnp.logical_or(k != a, a != c))
        def _():
            pl.semaphore_signal(barrier, inc=1, device_id=(k, a), device_id_type=MESH)
        return carry

    lax.fori_loop(0, 16, greet_rows, 0)

    def remote(src, dst, send, recv, device):
        return pltpu.make_async_remote_copy(src_ref=src, dst_ref=dst, send_sem=send, recv_sem=recv,
                                            device_id=device, device_id_type=MESH)

    def wait_bytes(ref, sem):
        pltpu.make_async_copy(ref, ref, sem).wait()

    pending = []

    def later(ref, sem, condition=None):
        pending.append((ref, sem, condition))

    def later_home(inside, outside, sem):
        later(inside, sem, home)
        later(outside, sem, jnp.logical_not(home))

    def wait_home(inside, outside, sem):
        pl.when(home)(functools.partial(wait_bytes, inside, sem))
        pl.when(jnp.logical_not(home))(functools.partial(wait_bytes, outside, sem))

    def drain():
        for ref, sem, condition in pending:
            if condition is None:
                wait_bytes(ref, sem)
            else:
                pl.when(condition)(functools.partial(wait_bytes, ref, sem))

    loads[1].wait()
    row = lax.broadcasted_iota(jnp.int32, (128, 128), 0)
    col = lax.broadcasted_iota(jnp.int32, (128, 128), 1)
    lead = lax.broadcasted_iota(jnp.int32, (1, 128), 1)
    filt = taps_v[...] + jnp.where(lead == 0, 1.0, 0.0)
    rolled = jnp.broadcast_to(filt, (128, 128))
    for bit in range(7):
        rolled = jnp.where((row // (1 << bit)) % 2 == 1, pltpu.roll(rolled, 1 << bit, 1), rolled)
    first = jnp.where(col >= row, rolled, 0.0)
    second = jnp.where(col < row, rolled, 0.0)
    high, low = split(jnp.concatenate([second, first], axis=0))
    w_high[...] = high
    w_low[...] = low
    high, low = split(jnp.concatenate([second.T, first.T], axis=1))
    filter_t[...] = jnp.concatenate([high, low], axis=0)

    loads[0].wait()
    @pl.when(a == c)
    def _():
        pl.semaphore_wait(barrier, 52)

    @pl.when(a != c)
    def _():
        pl.semaphore_wait(barrier, 53)

    def along_y(p, m, i):
        for ky in (1, 3, 2):
            target = ((y + ky) % 4) * 4 + ma
            remote(gather.at[p, m, y], gather.at[p, m, y], ag_send.at[p], ag_recv.at[p, i * 4 + ky], (target, c)).start()

    def gather_arc(p):
        own = gather.at[p, ma, y]
        remote(own, own, ag_send.at[p], ag_recv.at[p, 4], (y * 4 + (ma + 2) % 4, c)).start()
        along_y(p, ma, 0)
        remote(own, own, fwd_send.at[p], fwd_recv.at[p, 0], (sibling, c)).start()
        later(landed.at[0:2, 0:7], ag_send.at[p])

    def forward(p):
        wait_bytes(gather.at[p, (ma + 2) % 4, y], ag_recv.at[p, 4])
        along_y(p, (ma + 2) % 4, 1)

        def block_of(s):
            return ((xlo + s // 2) % 2) * 2 + (core + s % 2) % 2

        def finish(s):
            m = block_of(s)
            wait_bytes(pair_part.at[p, m], part_recv.at[p, m])
            for h in range(2):
                at = 2 * xh + h
                partial[p, m, at] = partial[p, m, at] + pair_part[p, m, h]

                @pl.when(4 * h + m != z)
                def _():
                    remote(partial.at[p, m, at], landed.at[p, (4 * h + m + 8 - z) % 8], rs_send.at[p], rs_recv.at[p],
                           (a, xh * 8 + 4 * h + m)).start()

        def step(s, carry):
            i, j = s // 2, s % 2
            m = block_of(s)

            @pl.when(j == 0)
            def _():
                for ky in range(4):
                    block = gather.at[p, m, (y + 4 - ky) % 4]
                    if ky == 0:
                        @pl.when(i > 0)
                        def _():
                            remote(block, block, fwd_send.at[p], fwd_recv.at[p, i], (sibling, c)).start()
                    else:
                        wait_bytes(block, ag_recv.at[p, i * 4 + ky])
                        remote(block, block, fwd_send.at[p], fwd_recv.at[p, i], (sibling, c)).start()

            @pl.when(j == 1)
            def _():
                wait_bytes(gather.at[p, m], fwd_recv.at[p, i])

            product = dot3(gather[p, m].reshape(64, 1024), t_high[...], t_low[...])
            partial[p, m] = product.reshape(4, 16, 512)
            remote(partial.at[p, m, pl.ds(2 - 2 * xh, 2)], pair_part.at[p, m], part_send.at[p], part_recv.at[p, m], (a, across)).start()

            @pl.when(s >= 2)
            def _():
                finish(s - 2)
            return carry

        lax.fori_loop(0, 4, step, 0)
        finish(2)
        finish(3)
        later(gather.at[p, 0:2], fwd_send.at[p])
        later(pair_part.at[p], part_send.at[p])
        later(landed.at[p, 1:8], rs_send.at[p])

    def forward_sum(p):
        wait_bytes(landed.at[p, 1:8], rs_recv.at[p])
        total = partial[p, mc, yc]
        for k in range(1, 8):
            total = total + landed[p, k]
        return total

    def columns(part):
        return pl.ds(0, 128) if part else pl.ds(128, 384)

    def gather_coef(it, part, value):
        at = columns(part)
        own, there = own_rows.at[it, :, at], back_rows.at[it, xlc, core, yc, :, at]
        own[...] = value

        @pl.when(home)
        def _():
            there[...] = value

        for dz in (4, 3, 5, 2, 6, 1, 7):
            remote(own, there, bg_send.at[it], bg_recv.at[it, part, dz, core],
                   (a - core + side, xh * 8 + (z + dz) % 8)).start()

        @pl.when(jnp.logical_not(home))
        def _():
            remote(own, there, bg_send.at[it], bg_recv.at[it, part, 0, core], (sibling, c)).start()

        if part == 1:
            later_home(landed.at[it, 1:8], landed.at[it], bg_send.at[it])

    def gather_coef_on(it):
        odd = (core + side) % 2
        for part in (0, 1):
            for n in (0, 2, 1, 3):
                for t in (0, 1):
                    dz = 2 * n + odd
                    source = (z + 8 - dz) % 8
                    block = back_rows.at[it, (source % 4) // 2, (core + t) % 2, 2 * xh + source // 4, :, columns(part)]
                    arrived = functools.partial(wait_bytes, block, bg_recv.at[it, part, dz, (core + t) % 2])
                    if n == 0 and t == 0:
                        pl.when(odd == 1)(arrived)
                    else:
                        arrived()
                    remote(block, block, bf_send.at[it], bf_recv.at[it], (a, across)).start()
        wait_bytes(back_rows.at[it, 0], bf_recv.at[it])
        later(back_rows.at[it, 0], bf_send.at[it])

    def spread(it, one, two):
        @pl.when(home)
        def _():
            own = vector.at[it, xlc, yc]
            own[...] = pack(one, two)

            def step(k, carry):
                remote(own, own, vec_send.at[it], vec_recv.at[it], (a, (c + k) % 16)).start()
                return carry

            lax.fori_loop(1, 16, step, 0)
        later(sum_dst.at[it, 1:16], vec_send.at[it], home)

    def spread_wait(it):
        wait_home(sum_dst.at[it, 1:8], sum_dst.at[it, 0:8], vec_recv.at[it])

    def spread_rows(it, xl, which):
        return jnp.concatenate([unpack(vector[it, xl, k], which) for k in range(4)], axis=0)

    def weighted_rows(it, xl, half):
        rows = back_rows[0, xl, half].reshape(64, 512)
        if it == 0:
            return rows * lax.rsqrt(1.0 + rows * rows * spread_rows(0, xl, 0))
        rows = rows - spread_rows(1, xl, 0) * back_rows[1, xl, half].reshape(64, 512)
        return rows * lax.rsqrt(1.0 + rows * rows * spread_rows(1, xl, 1))

    def backward(it):
        for i in (1, 0):
            xl = (xlo + i) % 2
            product = dot3(weighted_rows(it, xl, 0), g_high[0], g_low[0])
            product = product + dot3(weighted_rows(it, xl, 1), g_high[1], g_low[1])
            grad_part[it, xl] = product.reshape(4, 16, 1024)
            for ky in (2, 1, 3, 0):
                if ky == 0 and i == 0:
                    continue
                ty = (y + ky) % 4
                remote(grad_part.at[it, xl, ty], grad_land.at[it, i * 4 + ky], ra_send.at[it], ra_recv.at[it],
                       (ty * 4 + 2 * xl + core, c)).start()
        later(grad_land.at[it, 1:8], ra_send.at[it])

    def backward_sum(it):
        wait_bytes(grad_land.at[it, 1:8], ra_recv.at[it])
        total = grad_part[it, xlo, y]
        for k in range(1, 8):
            total = total + grad_land[it, k]
        return total

    def whiten(n, value, ahead=None):
        edge_src[n] = value[:, 384:512]

        @pl.when(a < 15)
        def _():
            remote(edge_src.at[n], edge_dst.at[n], edge_send.at[n], edge_recv.at[n], (a + 1, c)).start()

        later(edge_src.at[n], edge_send.at[n], a < 15)

        @pl.when(a == 0)
        def _():
            edge_dst[n] = jnp.zeros((16, 128), F32)

        inside = filter_blocks(jnp.concatenate([jnp.zeros((16, 128), F32), value], axis=1))
        inside = unblock(dot3(inside, w_high[...], w_low[...]))
        if ahead is not None:
            ahead(inside[:, 128:512])

        @pl.when(a > 0)
        def _():
            wait_bytes(edge_dst.at[n], edge_recv.at[n])

        outside = dot3(edge_dst[n], w_high[0:128, :], w_low[0:128, :])
        return jnp.concatenate([inside[:, 0:128] + outside, inside[:, 128:512]], axis=1)

    def time_sum(n, values, ahead=None):
        sum_src[n] = fold([lanes(value) for value in values])
        if ahead is not None:
            ahead()

        def step(k, carry):
            remote(sum_src.at[n], sum_dst.at[n, k], sum_send.at[n], sum_recv.at[n], ((a + k) % 16, c)).start()
            return carry

        lax.fori_loop(1, 16, step, 0)
        later(sum_dst.at[n, 1:16], sum_send.at[n])

    def time_sum_wait(n, count):
        wait_bytes(sum_dst.at[n, 1:16], sum_recv.at[n])
        total = sum_src[n]
        for k in range(1, 16):
            total = total + sum_dst[n, k]
        return unfold(total, count)

    def coef_sum(it, product, old):
        gp_src[it] = fold([lanes(product), lanes(old)])

        def step(k, carry):
            remote(gp_src.at[it], gp_dst.at[it, k], gp_send.at[it], gp_recv.at[it], (a, (c + k) % 16)).start()
            return carry

        lax.fori_loop(1, 16, step, 0)
        later(gp_dst.at[it, 1:16], gp_send.at[it])

    def coef_sum_wait(it):
        wait_bytes(gp_dst.at[it, 1:16], gp_recv.at[it])
        total = gp_src[it]
        for k in range(1, 16):
            total = total + gp_dst[it, k]

        @pl.when(a == c)
        def _():
            diag_gp[it] = total

            def step(k, carry):
                remote(diag_gp.at[it], diag_gp.at[it], diag_send.at[it], diag_recv.at[it], ((a + k) % 16, c)).start()
                return carry

            lax.fori_loop(1, 16, step, 0)
        later(gp_dst.at[it, 1:16], diag_send.at[it], a == c)
        return unfold(total, 2)

    def diag_gp_wait(it):
        @pl.when(a != c)
        def _():
            wait_bytes(diag_gp.at[it], diag_recv.at[it])
        return unfold(diag_gp[it], 2)

    def time_sum_rows():
        @pl.when(a == c)
        def _():
            cur_dst[a] = sum_src[ITERS]

        def step(k, carry):
            @pl.when(jnp.logical_or(c != a, k != c))
            def _():
                remote(sum_src.at[ITERS], cur_dst.at[a], cur_send, cur_recv, (c, k)).start()
            return carry

        lax.fori_loop(0, 16, step, 0)
        later(cur_dst.at[0:15], cur_send, a == c)
        later(cur_dst, cur_send, a != c)

    def time_sum_rows_wait():
        pl.when(a == c)(functools.partial(wait_bytes, cur_dst.at[0:15], cur_recv))
        pl.when(a != c)(functools.partial(wait_bytes, cur_dst, cur_recv))
        total = cur_dst[0]
        for k in range(1, 16):
            total = total + cur_dst[k]
        return unfold(total, 1)

    gather_arc(0)
    loads[2].wait()

    def prepare(r, carry):
        at = pl.ds(pl.multiple_of(r * 128, 128), 128)
        piece = design_f[at, :]
        high, low = split(piece)
        d_high[pl.ds(pl.multiple_of(r * 128 + 128, 128), 128), :] = high
        d_low[pl.ds(pl.multiple_of(r * 128 + 128, 128), 128), :] = low
        high, low = split(piece.T)
        t_high[:, at] = high
        t_low[:, at] = low
        return carry

    lax.fori_loop(0, 4, prepare, 0)
    forward(0)

    @pl.when(a < 15)
    def _():
        remote(design_f.at[384:512], halo, halo_sem.at[0], halo_sem.at[1], (a + 1, c)).start()

    later(halo, halo_sem.at[0], a < 15)

    @pl.when(a == 0)
    def _():
        halo[...] = jnp.zeros((128, 1024), F32)


    loads[3].wait()
    loads[4].wait()
    residual = obs_v[...] - forward_sum(0)
    whitened = whiten(0, residual, functools.partial(gather_coef, 0, 0))
    time_sum(0, [whitened * whitened])
    gather_coef(0, 1, whitened[:, 0:128])

    @pl.when(a > 0)
    def _():
        wait_bytes(halo, halo_sem.at[1])

    high, low = split(halo[...])
    d_high[0:128, :] = high
    d_low[0:128, :] = low

    def whiten_design(r, carry):
        at = pl.ds(pl.multiple_of(r * 128, 128), 256)
        both = jnp.dot(filter_t[...], d_high[at, :], preferred_element_type=F32)
        rest = jnp.dot(filter_t[0:128, :], d_low[at, :], preferred_element_type=F32)
        value = both[0:128] + both[128:256] + rest
        at = pl.ds(pl.multiple_of(r * 128, 128), 128)
        g_f[at, :] = value
        high, low = split(value)
        g_high[core, at, :] = high
        g_low[core, at, :] = low
        return carry

    lax.fori_loop(0, 4, whiten_design, 0)
    remote(g_f, g_s, design_sem.at[0], design_sem.at[1], (sibling, c)).start()
    later(g_f, design_sem.at[0])

    square, = time_sum_wait(0, 1)
    factor = 1.0 / (square * (HUBER_SQUARE / TOTAL_OBS) + EPSILON)
    spread(0, factor, factor)

    for it in range(ITERS):
        weights = lax.rsqrt(1.0 + whitened * whitened * factor)
        gather_coef_on(it)
        if it == 0:
            wait_bytes(g_s, design_sem.at[1])

            def split_sibling(r, carry):
                at = pl.ds(pl.multiple_of(r * 128, 128), 128)
                high, low = split(g_s[at, :])
                g_high[1 - core, at, :] = high
                g_low[1 - core, at, :] = low
                return carry

            lax.fori_loop(0, 4, split_sibling, 0)
        spread_wait(it)
        backward(it)
        gradient = backward_sum(it)
        conditioned = precond_v[...] * gradient
        gather[it + 1, ma, y] = conditioned
        gather_arc(it + 1)
        if it == 0:
            coef_sum(it, gradient * conditioned, gradient)
        else:
            coef_sum(it, gradient * conditioned, gradient * direction)
        forward(it + 1)
        gp_a, go_a = coef_sum_wait(it)
        if it == 0:
            first_direction = direction = conditioned
        else:
            beta = gp_a / gp_a_old
            direction = conditioned + beta * direction
            grad_dir = gp_a + beta * go_a
        image = forward_sum(it + 1)
        imaged = whiten(it + 1, image, functools.partial(gather_coef, 1, 0) if it == 0 else None)
        gp_c, go_c = diag_gp_wait(it)
        if it == 0:
            time_sum(1, [weights * imaged * imaged, whitened * imaged, imaged * imaged])
            gather_coef(1, 1, imaged[:, 0:128])
            curvature, cross, own = time_sum_wait(1, 3)
            alpha = gp_c / curvature
            square = jnp.maximum(square - 2.0 * alpha * cross + alpha * alpha * own, 0.0)
            factor = 1.0 / (square * (HUBER_SQUARE / TOTAL_OBS) + EPSILON)
            spread(1, alpha, factor)
            whitened = whitened - alpha * imaged
            gp_a_old, gp_c_old, image_old, imaged_old = gp_a, gp_c, image, imaged
        else:
            beta = gp_c / gp_c_old
            image = image + beta * image_old
            imaged = imaged + beta * imaged_old
            time_sum(2, [weights * imaged * imaged], time_sum_rows)
            curvature, = time_sum_wait(2, 1)
            alpha = (gp_c + beta * go_c) / curvature
        residual = residual - alpha * image
    out_ref[:, 1024:1536] = residual
    coefs = gather[0, ma, y] + unpack(vector[1, xlo, y], 0) * first_direction
    curvature, = time_sum_rows_wait()
    out_ref[:, 0:1024] = coefs + (grad_dir / curvature) * direction
    drain()


def body(design, observations, start_coefs, precond, taps):
    vmem = pl.BlockSpec(memory_space=pltpu.VMEM)
    dma = pltpu.SemaphoreType.DMA
    scratch = [
        pltpu.VMEM((512, 1024), F32),
        pltpu.VMEM((16, 512), F32), pltpu.VMEM((1, 1024), F32), pltpu.VMEM((1, 128), F32),
        pltpu.VMEM((128, 1024), F32),
        pltpu.VMEM((640, 1024), BF16), pltpu.VMEM((640, 1024), BF16),
        pltpu.VMEM((512, 1024), F32), pltpu.VMEM((512, 1024), F32),
        pltpu.VMEM((2, 512, 1024), BF16), pltpu.VMEM((2, 512, 1024), BF16),
        pltpu.VMEM((1024, 512), BF16), pltpu.VMEM((1024, 512), BF16),
        pltpu.VMEM((256, 128), BF16), pltpu.VMEM((256, 128), BF16), pltpu.VMEM((256, 256), BF16),
        pltpu.VMEM((3, 4, 4, 16, 1024), F32),
        pltpu.VMEM((3, 4, 4, 16, 512), F32),
        pltpu.VMEM((3, 4, 2, 16, 512), F32),
        pltpu.VMEM((3, 8, 16, 512), F32),
        pltpu.VMEM((2, 16, 512), F32),
        pltpu.VMEM((2, 2, 2, 4, 16, 512), F32),
        pltpu.VMEM((2, 2, 4, 16, 1024), F32),
        pltpu.VMEM((2, 8, 16, 1024), F32),
        pltpu.VMEM((3, 16, 128), F32), pltpu.VMEM((3, 16, 128), F32),
        pltpu.VMEM((3, 8, 128), F32), pltpu.VMEM((3, 16, 8, 128), F32),
        pltpu.VMEM((2, 8, 128), F32), pltpu.VMEM((2, 16, 8, 128), F32),
        pltpu.VMEM((2, 8, 128), F32), pltpu.VMEM((16, 8, 128), F32),
        pltpu.VMEM((2, 2, 4, 8, 128), F32),
        dma((5,)), dma((2,)), dma((2,)), dma, dma,
        dma((3,)), dma((3, 8)), dma((3,)), dma((3, 2)), dma((3,)), dma((3, 4)), dma((3,)), dma((3,)),
        dma((2,)), dma((2, 2, 8, 2)), dma((2,)), dma((2,)), dma((2,)), dma((2,)),
        dma((3,)), dma((3,)), dma((3,)), dma((3,)), dma((2,)), dma((2,)), dma((2,)), dma((2,)), dma((2,)), dma((2,)),
    ]
    out = pl.pallas_call(
        kernel,
        out_shape=jax.ShapeDtypeStruct((16, 1536), F32),
        in_specs=[pl.BlockSpec(memory_space=pltpu.HBM)] * 5,
        out_specs=vmem,
        scratch_shapes=scratch,
        compiler_params=pltpu.CompilerParams(collective_id=0, has_side_effects=True, vmem_limit_bytes=60 << 20),
    )(design, observations, start_coefs, precond.reshape(1, -1), taps.reshape(1, -1))
    return out[:, 0:1024], out[:, 1024:1536]


def solution(mesh):
    placed = (P("arc", "coef"), P("coef", "arc"), P("arc", "coef"), P("coef"), P())
    return jax.shard_map(
        body,
        mesh=mesh,
        in_specs=placed,
        out_specs=(P("arc", "coef"), P("coef", "arc")),
        check_vma=False,
    )
```

```python
import functools
import jax
import jax.numpy as jnp
from jax import lax
from jax.experimental import pallas as pl
from jax.experimental.pallas import tpu as pltpu
from jax.sharding import PartitionSpec as P

ITERS = 2
TOTAL_OBS = 8192
HUBER_SQUARE = 2.25
EPSILON = 1e-06

F32 = jnp.float32
BF16 = jnp.bfloat16
MESH = pl.DeviceIdType.MESH


def split(value):
    high = value.astype(BF16)
    low = (value - high.astype(F32)).astype(BF16)
    return high, low


def dot3(value, weight_high, weight_low):
    rows = value.shape[0]
    high, low = split(value)
    both = jnp.dot(jnp.concatenate([high, low], axis=0), weight_high, preferred_element_type=F32)
    rest = jnp.dot(high, weight_low, preferred_element_type=F32)
    return both[:rows] + both[rows:] + rest


def lanes(value):
    total = value[:, 0:128]
    for start in range(128, value.shape[1], 128):
        total = total + value[:, start:start + 128]
    return total


def fold(values):
    group = lax.broadcasted_iota(jnp.int32, (8, 128), 1) // 16
    tile = jnp.zeros((8, 128), F32)
    for n, value in enumerate(values):
        for shift in (64, 32, 16):
            value = value + pltpu.roll(value, shift, 1)
        tile = jnp.where(group == 2 * n, value[0:8], tile)
        tile = jnp.where(group == 2 * n + 1, value[8:16], tile)
    return tile


def unfold(tile, count):
    for shift in (8, 4, 2, 1):
        tile = tile + pltpu.roll(tile, shift, 1)
    return [jnp.concatenate([tile[:, 32 * n + 15:32 * n + 16], tile[:, 32 * n + 31:32 * n + 32]], axis=0) for n in range(count)]


def pack(one, two):
    lane = lax.broadcasted_iota(jnp.int32, (8, 128), 1)
    return jnp.where(lane < 64, jnp.where(lane < 32, one[0:8], one[8:16]), jnp.where(lane < 96, two[0:8], two[8:16]))


def unpack(tile, which):
    start = 64 * which
    return jnp.concatenate([tile[:, start:start + 1], tile[:, start + 32:start + 33]], axis=0)


def filter_blocks(extended):
    return jnp.concatenate([extended[:, j * 128:(j + 2) * 128] for j in range(4)], axis=0)


def unblock(value):
    return jnp.concatenate([value[j * 16:(j + 1) * 16] for j in range(4)], axis=1)


def kernel(design_hbm, obs_hbm, start_hbm, precond_hbm, taps_hbm, coefs_ref, misfit_ref,
           design_f, obs_v, precond_v, taps_v, halo, d_high, d_low, g_f, g_s, g_high, g_low, t_high, t_low, w_high, w_low, filter_t,
           gather, partial, pair_part, landed, own_rows, back_rows, grad_part, grad_land,
           edge_src, edge_dst, sum_src, sum_dst, gp_src, gp_dst, diag_gp, cur_dst, vector,
           load_sem, halo_sem, design_sem, cur_send, cur_recv, ag_send, ag_recv, fwd_send, fwd_recv, part_send, part_recv, rs_send, rs_recv,
           bg_send, bg_recv, bf_send, bf_recv, ra_send, ra_recv,
           edge_send, edge_recv, sum_send, sum_recv, gp_send, gp_recv, diag_send, diag_recv, vec_send, vec_recv):
    a = lax.axis_index("arc")
    c = lax.axis_index("coef")
    y, ma = a // 4, a % 4
    xlo, core = ma // 2, ma % 2
    xh, z = c // 8, c % 8
    yc, mc = c // 4, c % 4
    xlc, side = mc // 2, mc % 2
    sibling = a + 1 - 2 * core
    home = core == side
    across = (xh * 8 + 8) % 16 + z

    loads = []
    for n, (source, target) in enumerate([(start_hbm, gather.at[0, ma, y]), (taps_hbm, taps_v), (design_hbm, design_f),
                                          (obs_hbm, obs_v), (precond_hbm, precond_v)]):
        loads.append(pltpu.make_async_copy(source, target, load_sem.at[n]))
        loads[-1].start()

    barrier = pltpu.get_barrier_semaphore()

    def greet(k, carry):
        pl.semaphore_signal(barrier, inc=1, device_id=((a + k) % 16, c), device_id_type=MESH)
        pl.semaphore_signal(barrier, inc=1, device_id=(a, (c + k) % 16), device_id_type=MESH)
        return carry

    lax.fori_loop(1, 16, greet, 0)

    def greet_z(k, carry):
        pl.semaphore_signal(barrier, inc=1, device_id=(sibling, xh * 8 + (z + k) % 8), device_id_type=MESH)
        return carry

    lax.fori_loop(1, 8, greet_z, 0)

    def greet_rows(k, carry):
        @pl.when(jnp.logical_or(k != a, a != c))
        def _():
            pl.semaphore_signal(barrier, inc=1, device_id=(k, a), device_id_type=MESH)
        return carry

    lax.fori_loop(0, 16, greet_rows, 0)

    def remote(src, dst, send, recv, device):
        return pltpu.make_async_remote_copy(src_ref=src, dst_ref=dst, send_sem=send, recv_sem=recv,
                                            device_id=device, device_id_type=MESH)

    def wait_bytes(ref, sem):
        pltpu.make_async_copy(ref, ref, sem).wait()

    pending = []

    def later(ref, sem, condition=None):
        pending.append((ref, sem, condition))

    def later_home(inside, outside, sem):
        later(inside, sem, home)
        later(outside, sem, jnp.logical_not(home))

    def wait_home(inside, outside, sem):
        pl.when(home)(functools.partial(wait_bytes, inside, sem))
        pl.when(jnp.logical_not(home))(functools.partial(wait_bytes, outside, sem))

    def drain():
        for ref, sem, condition in pending:
            if condition is None:
                wait_bytes(ref, sem)
            else:
                pl.when(condition)(functools.partial(wait_bytes, ref, sem))

    loads[0].wait()
    @pl.when(a == c)
    def _():
        pl.semaphore_wait(barrier, 52)

    @pl.when(a != c)
    def _():
        pl.semaphore_wait(barrier, 53)

    def along_y(p, m, i):
        for ky in (1, 3, 2):
            target = ((y + ky) % 4) * 4 + ma
            remote(gather.at[p, m, y], gather.at[p, m, y], ag_send.at[p], ag_recv.at[p, i * 4 + ky], (target, c)).start()

    def gather_arc(p):
        own = gather.at[p, ma, y]
        remote(own, own, ag_send.at[p], ag_recv.at[p, 4], (y * 4 + (ma + 2) % 4, c)).start()
        along_y(p, ma, 0)
        remote(own, own, fwd_send.at[p], fwd_recv.at[p, 0], (sibling, c)).start()
        later(landed.at[0:2, 0:7], ag_send.at[p])

    def forward(p):
        wait_bytes(gather.at[p, (ma + 2) % 4, y], ag_recv.at[p, 4])
        along_y(p, (ma + 2) % 4, 1)

        def block_of(s):
            return ((xlo + s // 2) % 2) * 2 + (core + s % 2) % 2

        def finish(s):
            m = block_of(s)
            wait_bytes(pair_part.at[p, m], part_recv.at[p, m])
            for h in range(2):
                at = 2 * xh + h
                partial[p, m, at] = partial[p, m, at] + pair_part[p, m, h]

                @pl.when(4 * h + m != z)
                def _():
                    remote(partial.at[p, m, at], landed.at[p, (4 * h + m + 8 - z) % 8], rs_send.at[p], rs_recv.at[p],
                           (a, xh * 8 + 4 * h + m)).start()

        def step(s, carry):
            i, j = s // 2, s % 2
            m = block_of(s)

            @pl.when(j == 0)
            def _():
                for ky in range(4):
                    block = gather.at[p, m, (y + 4 - ky) % 4]
                    if ky == 0:
                        @pl.when(i > 0)
                        def _():
                            remote(block, block, fwd_send.at[p], fwd_recv.at[p, i], (sibling, c)).start()
                    else:
                        wait_bytes(block, ag_recv.at[p, i * 4 + ky])
                        remote(block, block, fwd_send.at[p], fwd_recv.at[p, i], (sibling, c)).start()

            @pl.when(j == 1)
            def _():
                wait_bytes(gather.at[p, m], fwd_recv.at[p, i])

            product = dot3(gather[p, m].reshape(64, 1024), t_high[...], t_low[...])
            partial[p, m] = product.reshape(4, 16, 512)
            remote(partial.at[p, m, pl.ds(2 - 2 * xh, 2)], pair_part.at[p, m], part_send.at[p], part_recv.at[p, m], (a, across)).start()

            @pl.when(s >= 2)
            def _():
                finish(s - 2)
            return carry

        lax.fori_loop(0, 4, step, 0)
        finish(2)
        finish(3)
        later(gather.at[p, 0:2], fwd_send.at[p])
        later(pair_part.at[p], part_send.at[p])
        later(landed.at[p, 1:8], rs_send.at[p])

    def forward_sum(p):
        wait_bytes(landed.at[p, 1:8], rs_recv.at[p])
        total = partial[p, mc, yc]
        for k in range(1, 8):
            total = total + landed[p, k]
        return total

    def columns(part):
        return pl.ds(0, 128) if part else pl.ds(128, 384)

    def gather_coef(it, part, value):
        at = columns(part)
        own, there = own_rows.at[it, :, at], back_rows.at[it, xlc, core, yc, :, at]
        own[...] = value

        @pl.when(home)
        def _():
            there[...] = value

        for dz in (4, 3, 5, 2, 6, 1, 7):
            remote(own, there, bg_send.at[it], bg_recv.at[it, part, dz, core],
                   (a - core + side, xh * 8 + (z + dz) % 8)).start()

        @pl.when(jnp.logical_not(home))
        def _():
            remote(own, there, bg_send.at[it], bg_recv.at[it, part, 0, core], (sibling, c)).start()

        if part == 1:
            later_home(landed.at[it, 1:8], landed.at[it], bg_send.at[it])

    def gather_coef_on(it):
        odd = (core + side) % 2
        for part in (0, 1):
            for n in (0, 2, 1, 3):
                for t in (0, 1):
                    dz = 2 * n + odd
                    source = (z + 8 - dz) % 8
                    block = back_rows.at[it, (source % 4) // 2, (core + t) % 2, 2 * xh + source // 4, :, columns(part)]
                    arrived = functools.partial(wait_bytes, block, bg_recv.at[it, part, dz, (core + t) % 2])
                    if n == 0 and t == 0:
                        pl.when(odd == 1)(arrived)
                    else:
                        arrived()
                    remote(block, block, bf_send.at[it], bf_recv.at[it], (a, across)).start()
        wait_bytes(back_rows.at[it, 0], bf_recv.at[it])
        later(back_rows.at[it, 0], bf_send.at[it])

    def spread(it, one, two):
        @pl.when(home)
        def _():
            own = vector.at[it, xlc, yc]
            own[...] = pack(one, two)

            def step(k, carry):
                remote(own, own, vec_send.at[it], vec_recv.at[it], (a, (c + k) % 16)).start()
                return carry

            lax.fori_loop(1, 16, step, 0)
        later(sum_dst.at[it, 1:16], vec_send.at[it], home)

    def spread_wait(it):
        wait_home(sum_dst.at[it, 1:8], sum_dst.at[it, 0:8], vec_recv.at[it])

    def spread_rows(it, xl, which):
        return jnp.concatenate([unpack(vector[it, xl, k], which) for k in range(4)], axis=0)

    def weighted_rows(it, xl, half):
        rows = back_rows[0, xl, half].reshape(64, 512)
        if it == 0:
            return rows * lax.rsqrt(1.0 + rows * rows * spread_rows(0, xl, 0))
        rows = rows - spread_rows(1, xl, 0) * back_rows[1, xl, half].reshape(64, 512)
        return rows * lax.rsqrt(1.0 + rows * rows * spread_rows(1, xl, 1))

    def backward(it):
        for i in (1, 0):
            xl = (xlo + i) % 2
            product = dot3(weighted_rows(it, xl, 0), g_high[0], g_low[0])
            product = product + dot3(weighted_rows(it, xl, 1), g_high[1], g_low[1])
            grad_part[it, xl] = product.reshape(4, 16, 1024)
            for ky in (2, 1, 3, 0):
                if ky == 0 and i == 0:
                    continue
                ty = (y + ky) % 4
                remote(grad_part.at[it, xl, ty], grad_land.at[it, i * 4 + ky], ra_send.at[it], ra_recv.at[it],
                       (ty * 4 + 2 * xl + core, c)).start()
        later(grad_land.at[it, 1:8], ra_send.at[it])

    def backward_sum(it):
        wait_bytes(grad_land.at[it, 1:8], ra_recv.at[it])
        total = grad_part[it, xlo, y]
        for k in range(1, 8):
            total = total + grad_land[it, k]
        return total

    def whiten(n, value, ahead=None):
        edge_src[n] = value[:, 384:512]

        @pl.when(a < 15)
        def _():
            remote(edge_src.at[n], edge_dst.at[n], edge_send.at[n], edge_recv.at[n], (a + 1, c)).start()

        later(edge_src.at[n], edge_send.at[n], a < 15)

        @pl.when(a == 0)
        def _():
            edge_dst[n] = jnp.zeros((16, 128), F32)

        inside = filter_blocks(jnp.concatenate([jnp.zeros((16, 128), F32), value], axis=1))
        inside = unblock(dot3(inside, w_high[...], w_low[...]))
        if ahead is not None:
            ahead(inside[:, 128:512])

        @pl.when(a > 0)
        def _():
            wait_bytes(edge_dst.at[n], edge_recv.at[n])

        outside = dot3(edge_dst[n], w_high[0:128, :], w_low[0:128, :])
        return jnp.concatenate([inside[:, 0:128] + outside, inside[:, 128:512]], axis=1)

    def time_sum(n, values):
        sum_src[n] = fold([lanes(value) for value in values])

        def step(k, carry):
            remote(sum_src.at[n], sum_dst.at[n, k], sum_send.at[n], sum_recv.at[n], ((a + k) % 16, c)).start()
            return carry

        lax.fori_loop(1, 16, step, 0)
        later(sum_dst.at[n, 1:16], sum_send.at[n])

    def time_sum_wait(n, count):
        wait_bytes(sum_dst.at[n, 1:16], sum_recv.at[n])
        total = sum_src[n]
        for k in range(1, 16):
            total = total + sum_dst[n, k]
        return unfold(total, count)

    def coef_sum(it, product, old):
        gp_src[it] = fold([lanes(product), lanes(old)])

        def step(k, carry):
            remote(gp_src.at[it], gp_dst.at[it, k], gp_send.at[it], gp_recv.at[it], (a, (c + k) % 16)).start()
            return carry

        lax.fori_loop(1, 16, step, 0)
        later(gp_dst.at[it, 1:16], gp_send.at[it])

    def coef_sum_wait(it):
        wait_bytes(gp_dst.at[it, 1:16], gp_recv.at[it])
        total = gp_src[it]
        for k in range(1, 16):
            total = total + gp_dst[it, k]

        @pl.when(a == c)
        def _():
            diag_gp[it] = total

            def step(k, carry):
                remote(diag_gp.at[it], diag_gp.at[it], diag_send.at[it], diag_recv.at[it], ((a + k) % 16, c)).start()
                return carry

            lax.fori_loop(1, 16, step, 0)
        later(gp_dst.at[it, 1:16], diag_send.at[it], a == c)
        return unfold(total, 2)

    def diag_gp_wait(it):
        @pl.when(a != c)
        def _():
            wait_bytes(diag_gp.at[it], diag_recv.at[it])
        return unfold(diag_gp[it], 2)

    def time_sum_rows():
        @pl.when(a == c)
        def _():
            cur_dst[a] = sum_src[ITERS]

        def step(k, carry):
            @pl.when(jnp.logical_or(c != a, k != c))
            def _():
                remote(sum_src.at[ITERS], cur_dst.at[a], cur_send, cur_recv, (c, k)).start()
            return carry

        lax.fori_loop(0, 16, step, 0)
        later(cur_dst.at[0:15], cur_send, a == c)
        later(cur_dst, cur_send, a != c)

    def time_sum_rows_wait():
        pl.when(a == c)(functools.partial(wait_bytes, cur_dst.at[0:15], cur_recv))
        pl.when(a != c)(functools.partial(wait_bytes, cur_dst, cur_recv))
        total = cur_dst[0]
        for k in range(1, 16):
            total = total + cur_dst[k]
        return unfold(total, 1)

    gather_arc(0)
    loads[2].wait()

    def prepare(r, carry):
        at = pl.ds(pl.multiple_of(r * 128, 128), 128)
        piece = design_f[at, :]
        high, low = split(piece)
        d_high[pl.ds(pl.multiple_of(r * 128 + 128, 128), 128), :] = high
        d_low[pl.ds(pl.multiple_of(r * 128 + 128, 128), 128), :] = low
        high, low = split(piece.T)
        t_high[:, at] = high
        t_low[:, at] = low
        return carry

    lax.fori_loop(0, 4, prepare, 0)
    forward(0)

    @pl.when(a < 15)
    def _():
        remote(design_f.at[384:512], halo, halo_sem.at[0], halo_sem.at[1], (a + 1, c)).start()

    later(halo, halo_sem.at[0], a < 15)

    @pl.when(a == 0)
    def _():
        halo[...] = jnp.zeros((128, 1024), F32)


    loads[1].wait()
    row = lax.broadcasted_iota(jnp.int32, (128, 128), 0)
    col = lax.broadcasted_iota(jnp.int32, (128, 128), 1)
    lead = lax.broadcasted_iota(jnp.int32, (1, 128), 1)
    filt = taps_v[...] + jnp.where(lead == 0, 1.0, 0.0)
    rolled = jnp.broadcast_to(filt, (128, 128))
    for bit in range(7):
        rolled = jnp.where((row // (1 << bit)) % 2 == 1, pltpu.roll(rolled, 1 << bit, 1), rolled)
    first = jnp.where(col >= row, rolled, 0.0)
    second = jnp.where(col < row, rolled, 0.0)
    high, low = split(jnp.concatenate([second, first], axis=0))
    w_high[...] = high
    w_low[...] = low
    high, low = split(jnp.concatenate([second.T, first.T], axis=1))
    filter_t[...] = jnp.concatenate([high, low], axis=0)

    loads[3].wait()
    loads[4].wait()
    residual = obs_v[...] - forward_sum(0)
    whitened = whiten(0, residual, functools.partial(gather_coef, 0, 0))
    time_sum(0, [whitened * whitened])
    gather_coef(0, 1, whitened[:, 0:128])

    @pl.when(a > 0)
    def _():
        wait_bytes(halo, halo_sem.at[1])

    high, low = split(halo[...])
    d_high[0:128, :] = high
    d_low[0:128, :] = low

    def whiten_design(r, carry):
        at = pl.ds(pl.multiple_of(r * 128, 128), 256)
        both = jnp.dot(filter_t[...], d_high[at, :], preferred_element_type=F32)
        rest = jnp.dot(filter_t[0:128, :], d_low[at, :], preferred_element_type=F32)
        value = both[0:128] + both[128:256] + rest
        at = pl.ds(pl.multiple_of(r * 128, 128), 128)
        g_f[at, :] = value
        high, low = split(value)
        g_high[core, at, :] = high
        g_low[core, at, :] = low
        return carry

    lax.fori_loop(0, 4, whiten_design, 0)
    remote(g_f, g_s, design_sem.at[0], design_sem.at[1], (sibling, c)).start()
    later(g_f, design_sem.at[0])

    square, = time_sum_wait(0, 1)
    factor = 1.0 / (square * (HUBER_SQUARE / TOTAL_OBS) + EPSILON)
    spread(0, factor, factor)

    for it in range(ITERS):
        weights = lax.rsqrt(1.0 + whitened * whitened * factor)
        gather_coef_on(it)
        if it == 0:
            wait_bytes(g_s, design_sem.at[1])

            def split_sibling(r, carry):
                at = pl.ds(pl.multiple_of(r * 128, 128), 128)
                high, low = split(g_s[at, :])
                g_high[1 - core, at, :] = high
                g_low[1 - core, at, :] = low
                return carry

            lax.fori_loop(0, 4, split_sibling, 0)
        spread_wait(it)
        backward(it)
        gradient = backward_sum(it)
        conditioned = precond_v[...] * gradient
        gather[it + 1, ma, y] = conditioned
        gather_arc(it + 1)
        if it == 0:
            coef_sum(it, gradient * conditioned, gradient)
        else:
            coef_sum(it, gradient * conditioned, gradient * direction)
        forward(it + 1)
        gp_a, go_a = coef_sum_wait(it)
        if it == 0:
            first_direction = direction = conditioned
        else:
            beta = gp_a / gp_a_old
            direction = conditioned + beta * direction
            grad_dir = gp_a + beta * go_a
        if it > 0:
            gp_c, go_c = diag_gp_wait(it)
        image = forward_sum(it + 1)
        imaged = whiten(it + 1, image, functools.partial(gather_coef, 1, 0) if it == 0 else None)
        if it == 0:
            time_sum(1, [weights * imaged * imaged, whitened * imaged, imaged * imaged])
            gather_coef(1, 1, imaged[:, 0:128])
            gp_c, go_c = diag_gp_wait(it)
            curvature, cross, own = time_sum_wait(1, 3)
            alpha = gp_c / curvature
            square = jnp.maximum(square - 2.0 * alpha * cross + alpha * alpha * own, 0.0)
            factor = 1.0 / (square * (HUBER_SQUARE / TOTAL_OBS) + EPSILON)
            spread(1, alpha, factor)
            whitened = whitened - alpha * imaged
            gp_a_old, gp_c_old, image_old, imaged_old = gp_a, gp_c, image, imaged
        else:
            beta = gp_c / gp_c_old
            image = image + beta * image_old
            imaged = imaged + beta * imaged_old
            time_sum(2, [weights * imaged * imaged])
            time_sum_rows()
            curvature, = time_sum_wait(2, 1)
            alpha = (gp_c + beta * go_c) / curvature
        residual = residual - alpha * image
    misfit_ref[...] = residual
    coefs = gather[0, ma, y] + unpack(vector[1, xlo, y], 0) * first_direction
    curvature, = time_sum_rows_wait()
    coefs_ref[...] = coefs + (grad_dir / curvature) * direction
    drain()


def body(design, observations, start_coefs, precond, taps):
    vmem = pl.BlockSpec(memory_space=pltpu.VMEM)
    dma = pltpu.SemaphoreType.DMA
    scratch = [
        pltpu.VMEM((512, 1024), F32),
        pltpu.VMEM((16, 512), F32), pltpu.VMEM((1, 1024), F32), pltpu.VMEM((1, 128), F32),
        pltpu.VMEM((128, 1024), F32),
        pltpu.VMEM((640, 1024), BF16), pltpu.VMEM((640, 1024), BF16),
        pltpu.VMEM((512, 1024), F32), pltpu.VMEM((512, 1024), F32),
        pltpu.VMEM((2, 512, 1024), BF16), pltpu.VMEM((2, 512, 1024), BF16),
        pltpu.VMEM((1024, 512), BF16), pltpu.VMEM((1024, 512), BF16),
        pltpu.VMEM((256, 128), BF16), pltpu.VMEM((256, 128), BF16), pltpu.VMEM((256, 256), BF16),
        pltpu.VMEM((3, 4, 4, 16, 1024), F32),
        pltpu.VMEM((3, 4, 4, 16, 512), F32),
        pltpu.VMEM((3, 4, 2, 16, 512), F32),
        pltpu.VMEM((3, 8, 16, 512), F32),
        pltpu.VMEM((2, 16, 512), F32),
        pltpu.VMEM((2, 2, 2, 4, 16, 512), F32),
        pltpu.VMEM((2, 2, 4, 16, 1024), F32),
        pltpu.VMEM((2, 8, 16, 1024), F32),
        pltpu.VMEM((3, 16, 128), F32), pltpu.VMEM((3, 16, 128), F32),
        pltpu.VMEM((3, 8, 128), F32), pltpu.VMEM((3, 16, 8, 128), F32),
        pltpu.VMEM((2, 8, 128), F32), pltpu.VMEM((2, 16, 8, 128), F32),
        pltpu.VMEM((2, 8, 128), F32), pltpu.VMEM((16, 8, 128), F32),
        pltpu.VMEM((2, 2, 4, 8, 128), F32),
        dma((5,)), dma((2,)), dma((2,)), dma, dma,
        dma((3,)), dma((3, 8)), dma((3,)), dma((3, 2)), dma((3,)), dma((3, 4)), dma((3,)), dma((3,)),
        dma((2,)), dma((2, 2, 8, 2)), dma((2,)), dma((2,)), dma((2,)), dma((2,)),
        dma((3,)), dma((3,)), dma((3,)), dma((3,)), dma((2,)), dma((2,)), dma((2,)), dma((2,)), dma((2,)), dma((2,)),
    ]
    return pl.pallas_call(
        kernel,
        out_shape=(jax.ShapeDtypeStruct(start_coefs.shape, F32), jax.ShapeDtypeStruct(observations.shape, F32)),
        in_specs=[pl.BlockSpec(memory_space=pltpu.HBM)] * 5,
        out_specs=(vmem, vmem),
        scratch_shapes=scratch,
        compiler_params=pltpu.CompilerParams(collective_id=0, has_side_effects=True, vmem_limit_bytes=60 << 20),
    )(design, observations, start_coefs, precond.reshape(1, -1), taps.reshape(1, -1))


def solution(mesh):
    placed = (P("arc", "coef"), P("coef", "arc"), P("arc", "coef"), P("coef"), P())
    return jax.shard_map(
        body,
        mesh=mesh,
        in_specs=placed,
        out_specs=(P("arc", "coef"), P("coef", "arc")),
        check_vma=False,
    )
```

```python
import functools
import jax
import jax.numpy as jnp
from jax import lax
from jax.experimental import pallas as pl
from jax.experimental.pallas import tpu as pltpu
from jax.sharding import PartitionSpec as P

ITERS = 2
TOTAL_OBS = 8192
HUBER_SQUARE = 2.25
EPSILON = 1e-06

F32 = jnp.float32
BF16 = jnp.bfloat16
MESH = pl.DeviceIdType.MESH


def split(value):
    high = value.astype(BF16)
    low = (value - high.astype(F32)).astype(BF16)
    return high, low


def dot3(value, weight_high, weight_low):
    rows = value.shape[0]
    high, low = split(value)
    both = jnp.dot(jnp.concatenate([high, low], axis=0), weight_high, preferred_element_type=F32)
    rest = jnp.dot(high, weight_low, preferred_element_type=F32)
    return both[:rows] + both[rows:] + rest


def lanes(value):
    total = value[:, 0:128]
    for start in range(128, value.shape[1], 128):
        total = total + value[:, start:start + 128]
    return total


def fold(values):
    group = lax.broadcasted_iota(jnp.int32, (8, 128), 1) // 16
    tile = jnp.zeros((8, 128), F32)
    for n, value in enumerate(values):
        for shift in (64, 32, 16):
            value = value + pltpu.roll(value, shift, 1)
        tile = jnp.where(group == 2 * n, value[0:8], tile)
        tile = jnp.where(group == 2 * n + 1, value[8:16], tile)
    return tile


def unfold(tile, count):
    for shift in (8, 4, 2, 1):
        tile = tile + pltpu.roll(tile, shift, 1)
    return [jnp.concatenate([tile[:, 32 * n + 15:32 * n + 16], tile[:, 32 * n + 31:32 * n + 32]], axis=0) for n in range(count)]


def pack(one, two):
    lane = lax.broadcasted_iota(jnp.int32, (8, 128), 1)
    return jnp.where(lane < 64, jnp.where(lane < 32, one[0:8], one[8:16]), jnp.where(lane < 96, two[0:8], two[8:16]))


def unpack(tile, which):
    start = 64 * which
    return jnp.concatenate([tile[:, start:start + 1], tile[:, start + 32:start + 33]], axis=0)


def filter_blocks(extended):
    return jnp.concatenate([extended[:, j * 128:(j + 2) * 128] for j in range(4)], axis=0)


def unblock(value):
    return jnp.concatenate([value[j * 16:(j + 1) * 16] for j in range(4)], axis=1)


def kernel(design_hbm, obs_hbm, start_hbm, precond_hbm, taps_hbm, coefs_ref, misfit_ref,
           design_f, obs_v, precond_v, taps_v, halo, d_high, d_low, g_f, g_s, g_high, g_low, t_high, t_low, w_high, w_low, filter_t,
           gather, partial, pair_part, landed, own_rows, back_rows, grad_part, grad_land,
           edge_src, edge_dst, sum_src, sum_dst, gp_src, gp_dst, diag_gp, cur_dst, vector,
           load_sem, halo_sem, design_sem, cur_send, cur_recv, ag_send, ag_recv, fwd_send, fwd_recv, part_send, part_recv, rs_send, rs_recv,
           bg_send, bg_recv, bf_send, bf_recv, ra_send, ra_recv,
           edge_send, edge_recv, sum_send, sum_recv, gp_send, gp_recv, diag_send, diag_recv, vec_send, vec_recv):
    a = lax.axis_index("arc")
    c = lax.axis_index("coef")
    y, ma = a // 4, a % 4
    xlo, core = ma // 2, ma % 2
    xh, z = c // 8, c % 8
    yc, mc = c // 4, c % 4
    xlc, side = mc // 2, mc % 2
    sibling = a + 1 - 2 * core
    home = core == side
    across = (xh * 8 + 8) % 16 + z

    loads = []
    for n, (source, target) in enumerate([(start_hbm, gather.at[0, ma, y]), (taps_hbm, taps_v), (design_hbm, design_f),
                                          (obs_hbm, obs_v), (precond_hbm, precond_v)]):
        loads.append(pltpu.make_async_copy(source, target, load_sem.at[n]))
        loads[-1].start()

    barrier = pltpu.get_barrier_semaphore()

    def greet(k, carry):
        pl.semaphore_signal(barrier, inc=1, device_id=((a + k) % 16, c), device_id_type=MESH)
        pl.semaphore_signal(barrier, inc=1, device_id=(a, (c + k) % 16), device_id_type=MESH)
        return carry

    lax.fori_loop(1, 16, greet, 0)

    def greet_z(k, carry):
        pl.semaphore_signal(barrier, inc=1, device_id=(sibling, xh * 8 + (z + k) % 8), device_id_type=MESH)
        return carry

    lax.fori_loop(1, 8, greet_z, 0)

    def greet_rows(k, carry):
        @pl.when(jnp.logical_or(k != a, a != c))
        def _():
            pl.semaphore_signal(barrier, inc=1, device_id=(k, a), device_id_type=MESH)
        return carry

    lax.fori_loop(0, 16, greet_rows, 0)

    def remote(src, dst, send, recv, device):
        return pltpu.make_async_remote_copy(src_ref=src, dst_ref=dst, send_sem=send, recv_sem=recv,
                                            device_id=device, device_id_type=MESH)

    def wait_bytes(ref, sem):
        pltpu.make_async_copy(ref, ref, sem).wait()

    pending = []

    def later(ref, sem, condition=None):
        pending.append((ref, sem, condition))

    def later_home(inside, outside, sem):
        later(inside, sem, home)
        later(outside, sem, jnp.logical_not(home))

    def wait_home(inside, outside, sem):
        pl.when(home)(functools.partial(wait_bytes, inside, sem))
        pl.when(jnp.logical_not(home))(functools.partial(wait_bytes, outside, sem))

    def drain():
        for ref, sem, condition in pending:
            if condition is None:
                wait_bytes(ref, sem)
            else:
                pl.when(condition)(functools.partial(wait_bytes, ref, sem))

    loads[0].wait()
    @pl.when(a == c)
    def _():
        pl.semaphore_wait(barrier, 52)

    @pl.when(a != c)
    def _():
        pl.semaphore_wait(barrier, 53)

    def along_y(p, m, i):
        for ky in (1, 3, 2):
            target = ((y + ky) % 4) * 4 + ma
            remote(gather.at[p, m, y], gather.at[p, m, y], ag_send.at[p], ag_recv.at[p, i * 4 + ky], (target, c)).start()

    def gather_arc(p):
        own = gather.at[p, ma, y]
        remote(own, own, ag_send.at[p], ag_recv.at[p, 4], (y * 4 + (ma + 2) % 4, c)).start()
        along_y(p, ma, 0)
        remote(own, own, fwd_send.at[p], fwd_recv.at[p, 0], (sibling, c)).start()
        later(landed.at[0:2, 0:7], ag_send.at[p])

    def forward(p):
        wait_bytes(gather.at[p, (ma + 2) % 4, y], ag_recv.at[p, 4])
        along_y(p, (ma + 2) % 4, 1)

        def block_of(s):
            return ((xlo + s // 2) % 2) * 2 + (core + s % 2) % 2

        def finish(s):
            m = block_of(s)
            wait_bytes(pair_part.at[p, m], part_recv.at[p, m])
            for h in range(2):
                at = 2 * xh + h
                partial[p, m, at] = partial[p, m, at] + pair_part[p, m, h]

                @pl.when(4 * h + m != z)
                def _():
                    remote(partial.at[p, m, at], landed.at[p, (4 * h + m + 8 - z) % 8], rs_send.at[p], rs_recv.at[p],
                           (a, xh * 8 + 4 * h + m)).start()

        def step(s, carry):
            i, j = s // 2, s % 2
            m = block_of(s)

            @pl.when(j == 0)
            def _():
                for ky in range(4):
                    block = gather.at[p, m, (y + 4 - ky) % 4]
                    if ky == 0:
                        @pl.when(i > 0)
                        def _():
                            remote(block, block, fwd_send.at[p], fwd_recv.at[p, i], (sibling, c)).start()
                    else:
                        wait_bytes(block, ag_recv.at[p, i * 4 + ky])
                        remote(block, block, fwd_send.at[p], fwd_recv.at[p, i], (sibling, c)).start()

            @pl.when(j == 1)
            def _():
                wait_bytes(gather.at[p, m], fwd_recv.at[p, i])

            product = dot3(gather[p, m].reshape(64, 1024), t_high[...], t_low[...])
            partial[p, m] = product.reshape(4, 16, 512)
            remote(partial.at[p, m, pl.ds(2 - 2 * xh, 2)], pair_part.at[p, m], part_send.at[p], part_recv.at[p, m], (a, across)).start()

            @pl.when(s >= 2)
            def _():
                finish(s - 2)
            return carry

        lax.fori_loop(0, 4, step, 0)
        finish(2)
        finish(3)
        later(gather.at[p, 0:2], fwd_send.at[p])
        later(pair_part.at[p], part_send.at[p])
        later(landed.at[p, 1:8], rs_send.at[p])

    def forward_sum(p):
        wait_bytes(landed.at[p, 1:8], rs_recv.at[p])
        total = partial[p, mc, yc]
        for k in range(1, 8):
            total = total + landed[p, k]
        return total

    def columns(part):
        return pl.ds(0, 128) if part else pl.ds(128, 384)

    def gather_coef(it, part, value):
        at = columns(part)
        own, there = own_rows.at[it, :, at], back_rows.at[it, xlc, core, yc, :, at]
        own[...] = value

        @pl.when(home)
        def _():
            there[...] = value

        for dz in (4, 3, 5, 2, 6, 1, 7):
            remote(own, there, bg_send.at[it], bg_recv.at[it, part, dz, core],
                   (a - core + side, xh * 8 + (z + dz) % 8)).start()

        @pl.when(jnp.logical_not(home))
        def _():
            remote(own, there, bg_send.at[it], bg_recv.at[it, part, 0, core], (sibling, c)).start()

        if part == 1:
            later_home(landed.at[it, 1:8], landed.at[it], bg_send.at[it])

    def pass_on(it, part, steps):
        odd = (core + side) % 2
        for n in steps:
            for t in (0, 1):
                dz = 2 * n + odd
                source = (z + 8 - dz) % 8
                block = back_rows.at[it, (source % 4) // 2, (core + t) % 2, 2 * xh + source // 4, :, columns(part)]
                arrived = functools.partial(wait_bytes, block, bg_recv.at[it, part, dz, (core + t) % 2])
                if n == 0 and t == 0:
                    pl.when(odd == 1)(arrived)
                else:
                    arrived()
                remote(block, block, bf_send.at[it], bf_recv.at[it], (a, across)).start()

    def gather_coef_on(it):
        pass_on(it, 0, (1, 3))
        pass_on(it, 1, (0, 2, 1, 3))
        wait_bytes(back_rows.at[it, 0], bf_recv.at[it])
        later(back_rows.at[it, 0], bf_send.at[it])

    def spread(it, one, two):
        @pl.when(home)
        def _():
            own = vector.at[it, xlc, yc]
            own[...] = pack(one, two)

            def step(k, carry):
                remote(own, own, vec_send.at[it], vec_recv.at[it], (a, (c + k) % 16)).start()
                return carry

            lax.fori_loop(1, 16, step, 0)
        later(sum_dst.at[it, 1:16], vec_send.at[it], home)

    def spread_wait(it):
        wait_home(sum_dst.at[it, 1:8], sum_dst.at[it, 0:8], vec_recv.at[it])

    def spread_rows(it, xl, which):
        return jnp.concatenate([unpack(vector[it, xl, k], which) for k in range(4)], axis=0)

    def weighted_rows(it, xl, half):
        rows = back_rows[0, xl, half].reshape(64, 512)
        if it == 0:
            return rows * lax.rsqrt(1.0 + rows * rows * spread_rows(0, xl, 0))
        rows = rows - spread_rows(1, xl, 0) * back_rows[1, xl, half].reshape(64, 512)
        return rows * lax.rsqrt(1.0 + rows * rows * spread_rows(1, xl, 1))

    def backward(it):
        for i in (1, 0):
            xl = (xlo + i) % 2
            product = dot3(weighted_rows(it, xl, 0), g_high[0], g_low[0])
            product = product + dot3(weighted_rows(it, xl, 1), g_high[1], g_low[1])
            grad_part[it, xl] = product.reshape(4, 16, 1024)
            for ky in (2, 1, 3, 0):
                if ky == 0 and i == 0:
                    continue
                ty = (y + ky) % 4
                remote(grad_part.at[it, xl, ty], grad_land.at[it, i * 4 + ky], ra_send.at[it], ra_recv.at[it],
                       (ty * 4 + 2 * xl + core, c)).start()
        later(grad_land.at[it, 1:8], ra_send.at[it])

    def backward_sum(it):
        wait_bytes(grad_land.at[it, 1:8], ra_recv.at[it])
        total = grad_part[it, xlo, y]
        for k in range(1, 8):
            total = total + grad_land[it, k]
        return total

    def whiten(n, value, ahead=None):
        edge_src[n] = value[:, 384:512]

        @pl.when(a < 15)
        def _():
            remote(edge_src.at[n], edge_dst.at[n], edge_send.at[n], edge_recv.at[n], (a + 1, c)).start()

        later(edge_src.at[n], edge_send.at[n], a < 15)

        @pl.when(a == 0)
        def _():
            edge_dst[n] = jnp.zeros((16, 128), F32)

        inside = filter_blocks(jnp.concatenate([jnp.zeros((16, 128), F32), value], axis=1))
        inside = unblock(dot3(inside, w_high[...], w_low[...]))
        if ahead is not None:
            ahead(inside[:, 128:512])

        @pl.when(a > 0)
        def _():
            wait_bytes(edge_dst.at[n], edge_recv.at[n])

        outside = dot3(edge_dst[n], w_high[0:128, :], w_low[0:128, :])
        return jnp.concatenate([inside[:, 0:128] + outside, inside[:, 128:512]], axis=1)

    def time_sum(n, values):
        sum_src[n] = fold([lanes(value) for value in values])

        def step(k, carry):
            remote(sum_src.at[n], sum_dst.at[n, k], sum_send.at[n], sum_recv.at[n], ((a + k) % 16, c)).start()
            return carry

        lax.fori_loop(1, 16, step, 0)
        later(sum_dst.at[n, 1:16], sum_send.at[n])

    def time_sum_wait(n, count):
        wait_bytes(sum_dst.at[n, 1:16], sum_recv.at[n])
        total = sum_src[n]
        for k in range(1, 16):
            total = total + sum_dst[n, k]
        return unfold(total, count)

    def coef_sum(it, product, old):
        gp_src[it] = fold([lanes(product), lanes(old)])

        def step(k, carry):
            remote(gp_src.at[it], gp_dst.at[it, k], gp_send.at[it], gp_recv.at[it], (a, (c + k) % 16)).start()
            return carry

        lax.fori_loop(1, 16, step, 0)
        later(gp_dst.at[it, 1:16], gp_send.at[it])

    def coef_sum_wait(it):
        wait_bytes(gp_dst.at[it, 1:16], gp_recv.at[it])
        total = gp_src[it]
        for k in range(1, 16):
            total = total + gp_dst[it, k]

        @pl.when(a == c)
        def _():
            diag_gp[it] = total

            def step(k, carry):
                remote(diag_gp.at[it], diag_gp.at[it], diag_send.at[it], diag_recv.at[it], ((a + k) % 16, c)).start()
                return carry

            lax.fori_loop(1, 16, step, 0)
        later(gp_dst.at[it, 1:16], diag_send.at[it], a == c)
        return unfold(total, 2)

    def diag_gp_wait(it):
        @pl.when(a != c)
        def _():
            wait_bytes(diag_gp.at[it], diag_recv.at[it])
        return unfold(diag_gp[it], 2)

    def time_sum_rows():
        @pl.when(a == c)
        def _():
            cur_dst[a] = sum_src[ITERS]

        def step(k, carry):
            @pl.when(jnp.logical_or(c != a, k != c))
            def _():
                remote(sum_src.at[ITERS], cur_dst.at[a], cur_send, cur_recv, (c, k)).start()
            return carry

        lax.fori_loop(0, 16, step, 0)
        later(cur_dst.at[0:15], cur_send, a == c)
        later(cur_dst, cur_send, a != c)

    def time_sum_rows_wait():
        pl.when(a == c)(functools.partial(wait_bytes, cur_dst.at[0:15], cur_recv))
        pl.when(a != c)(functools.partial(wait_bytes, cur_dst, cur_recv))
        total = cur_dst[0]
        for k in range(1, 16):
            total = total + cur_dst[k]
        return unfold(total, 1)

    gather_arc(0)
    loads[2].wait()

    def prepare(r, carry):
        at = pl.ds(pl.multiple_of(r * 128, 128), 128)
        piece = design_f[at, :]
        high, low = split(piece)
        d_high[pl.ds(pl.multiple_of(r * 128 + 128, 128), 128), :] = high
        d_low[pl.ds(pl.multiple_of(r * 128 + 128, 128), 128), :] = low
        high, low = split(piece.T)
        t_high[:, at] = high
        t_low[:, at] = low
        return carry

    lax.fori_loop(0, 4, prepare, 0)
    forward(0)

    @pl.when(a < 15)
    def _():
        remote(design_f.at[384:512], halo, halo_sem.at[0], halo_sem.at[1], (a + 1, c)).start()

    later(halo, halo_sem.at[0], a < 15)

    @pl.when(a == 0)
    def _():
        halo[...] = jnp.zeros((128, 1024), F32)


    loads[1].wait()
    row = lax.broadcasted_iota(jnp.int32, (128, 128), 0)
    col = lax.broadcasted_iota(jnp.int32, (128, 128), 1)
    lead = lax.broadcasted_iota(jnp.int32, (1, 128), 1)
    filt = taps_v[...] + jnp.where(lead == 0, 1.0, 0.0)
    rolled = jnp.broadcast_to(filt, (128, 128))
    for bit in range(7):
        rolled = jnp.where((row // (1 << bit)) % 2 == 1, pltpu.roll(rolled, 1 << bit, 1), rolled)
    first = jnp.where(col >= row, rolled, 0.0)
    second = jnp.where(col < row, rolled, 0.0)
    high, low = split(jnp.concatenate([second, first], axis=0))
    w_high[...] = high
    w_low[...] = low
    high, low = split(jnp.concatenate([second.T, first.T], axis=1))
    filter_t[...] = jnp.concatenate([high, low], axis=0)

    loads[3].wait()
    loads[4].wait()
    residual = obs_v[...] - forward_sum(0)
    whitened = whiten(0, residual, functools.partial(gather_coef, 0, 0))
    time_sum(0, [whitened * whitened])
    gather_coef(0, 1, whitened[:, 0:128])

    @pl.when(a > 0)
    def _():
        wait_bytes(halo, halo_sem.at[1])

    high, low = split(halo[...])
    d_high[0:128, :] = high
    d_low[0:128, :] = low

    def whiten_design(r, carry):
        at = pl.ds(pl.multiple_of(r * 128, 128), 256)
        both = jnp.dot(filter_t[...], d_high[at, :], preferred_element_type=F32)
        rest = jnp.dot(filter_t[0:128, :], d_low[at, :], preferred_element_type=F32)
        value = both[0:128] + both[128:256] + rest
        at = pl.ds(pl.multiple_of(r * 128, 128), 128)
        g_f[at, :] = value
        high, low = split(value)
        g_high[core, at, :] = high
        g_low[core, at, :] = low
        return carry

    lax.fori_loop(0, 4, whiten_design, 0)
    remote(g_f, g_s, design_sem.at[0], design_sem.at[1], (sibling, c)).start()
    later(g_f, design_sem.at[0])

    pass_on(0, 0, (0, 2))
    square, = time_sum_wait(0, 1)
    factor = 1.0 / (square * (HUBER_SQUARE / TOTAL_OBS) + EPSILON)
    spread(0, factor, factor)

    for it in range(ITERS):
        weights = lax.rsqrt(1.0 + whitened * whitened * factor)
        gather_coef_on(it)
        if it == 0:
            wait_bytes(g_s, design_sem.at[1])

            def split_sibling(r, carry):
                at = pl.ds(pl.multiple_of(r * 128, 128), 128)
                high, low = split(g_s[at, :])
                g_high[1 - core, at, :] = high
                g_low[1 - core, at, :] = low
                return carry

            lax.fori_loop(0, 4, split_sibling, 0)
        spread_wait(it)
        backward(it)
        gradient = backward_sum(it)
        conditioned = precond_v[...] * gradient
        gather[it + 1, ma, y] = conditioned
        gather_arc(it + 1)
        if it == 0:
            coef_sum(it, gradient * conditioned, gradient)
        else:
            coef_sum(it, gradient * conditioned, gradient * direction)
        forward(it + 1)
        gp_a, go_a = coef_sum_wait(it)
        if it == 0:
            first_direction = direction = conditioned
        else:
            beta = gp_a / gp_a_old
            direction = conditioned + beta * direction
            grad_dir = gp_a + beta * go_a
        if it > 0:
            gp_c, go_c = diag_gp_wait(it)
        image = forward_sum(it + 1)
        imaged = whiten(it + 1, image, functools.partial(gather_coef, 1, 0) if it == 0 else None)
        if it == 0:
            time_sum(1, [weights * imaged * imaged, whitened * imaged, imaged * imaged])
            gather_coef(1, 1, imaged[:, 0:128])
            pass_on(1, 0, (0, 2))
            gp_c, go_c = diag_gp_wait(it)
            curvature, cross, own = time_sum_wait(1, 3)
            alpha = gp_c / curvature
            square = jnp.maximum(square - 2.0 * alpha * cross + alpha * alpha * own, 0.0)
            factor = 1.0 / (square * (HUBER_SQUARE / TOTAL_OBS) + EPSILON)
            spread(1, alpha, factor)
            whitened = whitened - alpha * imaged
            gp_a_old, gp_c_old, image_old, imaged_old = gp_a, gp_c, image, imaged
        else:
            beta = gp_c / gp_c_old
            image = image + beta * image_old
            imaged = imaged + beta * imaged_old
            time_sum(2, [weights * imaged * imaged])
            time_sum_rows()
            curvature, = time_sum_wait(2, 1)
            alpha = (gp_c + beta * go_c) / curvature
        residual = residual - alpha * image
    misfit_ref[...] = residual
    coefs = gather[0, ma, y] + unpack(vector[1, xlo, y], 0) * first_direction
    curvature, = time_sum_rows_wait()
    coefs_ref[...] = coefs + (grad_dir / curvature) * direction
    drain()


def body(design, observations, start_coefs, precond, taps):
    vmem = pl.BlockSpec(memory_space=pltpu.VMEM)
    dma = pltpu.SemaphoreType.DMA
    scratch = [
        pltpu.VMEM((512, 1024), F32),
        pltpu.VMEM((16, 512), F32), pltpu.VMEM((1, 1024), F32), pltpu.VMEM((1, 128), F32),
        pltpu.VMEM((128, 1024), F32),
        pltpu.VMEM((640, 1024), BF16), pltpu.VMEM((640, 1024), BF16),
        pltpu.VMEM((512, 1024), F32), pltpu.VMEM((512, 1024), F32),
        pltpu.VMEM((2, 512, 1024), BF16), pltpu.VMEM((2, 512, 1024), BF16),
        pltpu.VMEM((1024, 512), BF16), pltpu.VMEM((1024, 512), BF16),
        pltpu.VMEM((256, 128), BF16), pltpu.VMEM((256, 128), BF16), pltpu.VMEM((256, 256), BF16),
        pltpu.VMEM((3, 4, 4, 16, 1024), F32),
        pltpu.VMEM((3, 4, 4, 16, 512), F32),
        pltpu.VMEM((3, 4, 2, 16, 512), F32),
        pltpu.VMEM((3, 8, 16, 512), F32),
        pltpu.VMEM((2, 16, 512), F32),
        pltpu.VMEM((2, 2, 2, 4, 16, 512), F32),
        pltpu.VMEM((2, 2, 4, 16, 1024), F32),
        pltpu.VMEM((2, 8, 16, 1024), F32),
        pltpu.VMEM((3, 16, 128), F32), pltpu.VMEM((3, 16, 128), F32),
        pltpu.VMEM((3, 8, 128), F32), pltpu.VMEM((3, 16, 8, 128), F32),
        pltpu.VMEM((2, 8, 128), F32), pltpu.VMEM((2, 16, 8, 128), F32),
        pltpu.VMEM((2, 8, 128), F32), pltpu.VMEM((16, 8, 128), F32),
        pltpu.VMEM((2, 2, 4, 8, 128), F32),
        dma((5,)), dma((2,)), dma((2,)), dma, dma,
        dma((3,)), dma((3, 8)), dma((3,)), dma((3, 2)), dma((3,)), dma((3, 4)), dma((3,)), dma((3,)),
        dma((2,)), dma((2, 2, 8, 2)), dma((2,)), dma((2,)), dma((2,)), dma((2,)),
        dma((3,)), dma((3,)), dma((3,)), dma((3,)), dma((2,)), dma((2,)), dma((2,)), dma((2,)), dma((2,)), dma((2,)),
    ]
    return pl.pallas_call(
        kernel,
        out_shape=(jax.ShapeDtypeStruct(start_coefs.shape, F32), jax.ShapeDtypeStruct(observations.shape, F32)),
        in_specs=[pl.BlockSpec(memory_space=pltpu.HBM)] * 5,
        out_specs=(vmem, vmem),
        scratch_shapes=scratch,
        compiler_params=pltpu.CompilerParams(collective_id=0, has_side_effects=True, vmem_limit_bytes=60 << 20),
    )(design, observations, start_coefs, precond.reshape(1, -1), taps.reshape(1, -1))


def solution(mesh):
    placed = (P("arc", "coef"), P("coef", "arc"), P("arc", "coef"), P("coef"), P())
    return jax.shard_map(
        body,
        mesh=mesh,
        in_specs=placed,
        out_specs=(P("arc", "coef"), P("coef", "arc")),
        check_vma=False,
    )
```
